512 devices in a mesh: leaf: 32 (over z, core), blk: 16 (over y, x).
Axes of the slice: x: 4, y: 4, z: 16, core: 2. Of those that a mesh axis runs over, the one named last changes fastest.
Arguments:
- rhs_local: float32 [262144, 32], P(('leaf', 'blk')), may hold values from -6 to 6
- inv_local: float32 [262144, 512], P(('leaf', 'blk'))
- couple_local: float32 [262144, 1536], P(('leaf', 'blk')), may hold values from -0.02734375 to 0.02734375
- row_index: int32 [512, 1536], P(('leaf', 'blk')), may hold values from 0 to 8191, as said below
- rhs_sep1: float32 [8192, 32], P(('leaf', 'blk')), may hold values from -6 to 6
- inv_sep1: float32 [8192, 4096], P(('leaf', 'blk'))
- couple_sep1: float32 [8192, 4096], P(('leaf', 'blk')), may hold values from -0.0625 to 0.0625
- rhs_sep0: float32 [4096, 32], P(('leaf', 'blk')), may hold values from -6 to 6
- inv_sep0: float32 [4096, 4096], P(('leaf', 'blk'))
Outputs:
- x_local: float32 [262144, 32], P(('leaf', 'blk'))
- x_sep1: float32 [8192, 32], P(('leaf', 'blk'))
- x_sep0: float32 [4096, 32], P(('leaf', 'blk'))
The draws below stay inside these ranges and needn't reach their ends.
Inputs may be any that keep to these rules, and one draw needn't show every extreme that they name: `row_index`: row d lists 1536 distinct rows in increasing order among the 8192 rows of device-local supernode d's ancestors (its level-1 separator, then the root, 4096 rows each); it always holds the first and the last of them.
All inputs are finite; a program needn't handle non-finite values.
Results may differ from the reference program's by a relative error of at most 0.00013.
Values sent between devices are 32-bit elements; how exact they have to be, the bound alone decides.
No kernel may reach another device: no remote copies, remote signals or barrier semaphores. Data moves between devices by JAX's collectives and lax.ppermute only.
A program may use at most 64 MiB of HBM per device.

```python
import math
import jax
import jax.numpy as jnp
from jax import lax

S = 4096
SD = 512
K = 1536
R = 32
LOCALS = 512
N_LEAF = 32
N_BLK = 16


def lower_blocks(key, blocks, order, log_low, log_high, spread):
    lower_key, diag_key = jax.random.split(key)
    lower = jax.random.normal(lower_key, (blocks, order, order), jnp.float32) * (spread / math.sqrt(order))
    diagonal = jnp.exp(jax.random.uniform(diag_key, (blocks, order), jnp.float32, log_low, log_high))
    rows = jnp.arange(order)[:, None]
    cols = jnp.arange(order)[None, :]
    strict = jnp.where(rows > cols, lower, 0.0)
    return strict + jnp.where(rows == cols, diagonal[:, :, None], 0.0)


def draw_inv_local(key, part):
    key = jax.random.fold_in(key, 11)
    blocks = lower_blocks(key, N_LEAF * N_BLK, SD, math.log(0.8), math.log(1.25), 0.6)
    return blocks.reshape(N_LEAF * N_BLK * SD, SD)


def draw_inv_sep1(key, part):
    key = jax.random.fold_in(key, 13)
    blocks = lower_blocks(key, 2, S, math.log(0.8), math.log(1.25), 0.6)
    return blocks.reshape(2 * S, S)


def draw_inv_sep0(key, part):
    key = jax.random.fold_in(key, 14)
    blocks = lower_blocks(key, 1, S, math.log(0.8), math.log(1.25), 0.6)
    return blocks.reshape(S, S)


def draw_row_index(key, part):
    key = jax.random.fold_in(key, 7)
    keys = jax.random.split(key, N_LEAF * N_BLK)

    def one_row(row_key):
        inner = jax.random.permutation(row_key, 2 * S - 2)[:K - 2].astype(jnp.int32) + 1
        first = jnp.zeros((1,), jnp.int32)
        final = jnp.full((1,), 2 * S - 1, jnp.int32)
        return jnp.concatenate([first, jnp.sort(inner), final])
    return jax.vmap(one_row)(keys)


def block_scale(key, dims, cuts, low, top_value):
    level = 1.0
    for position, parts in cuts:
        draws = jax.random.uniform(jax.random.fold_in(jax.random.fold_in(key, 6), position), (parts,), jnp.float32, low / len(cuts), top_value / len(cuts))
        level = level * jnp.repeat(jnp.exp(draws), dims[position] // parts).reshape((-1,) + (1,) * (len(dims) - 1 - position))
    return level


def gaussian(key, shape, scale, most, cuts=(), kind=jnp.bfloat16):
    loudness = block_scale(key, shape, cuts, -0.22, 0.18) if cuts else 1.0
    result = jax.random.normal(key, shape, jnp.float32) * scale * loudness
    return jnp.minimum(jnp.maximum(result, -most), most).astype(kind)


def setup_inputs(seed: int = 0) -> dict:
    streams_of = jax.random.split(jax.random.key(seed), 10)
    rhs_local = gaussian(streams_of[0], (LOCALS * SD, R), 1.0, 6.0, ((0, 512),), jnp.float32)
    inv_local = draw_inv_local(jax.random.fold_in(streams_of[9], 71), 0)
    couple_local = gaussian(streams_of[2], (LOCALS * SD, K), (LOCALS * SD * K // (2 * S)) ** -0.5, 0.02734375, ((0, 512),), jnp.float32)
    row_index = draw_row_index(jax.random.fold_in(streams_of[9], 71), 0)
    rhs_sep1 = gaussian(streams_of[4], (2 * S, R), 1.0, 6.0, ((0, 512),), jnp.float32)
    inv_sep1 = draw_inv_sep1(jax.random.fold_in(streams_of[9], 71), 0)
    couple_sep1 = gaussian(streams_of[6], (2 * S, S), (2 * S) ** -0.5, 0.0625, ((0, 512),), jnp.float32)
    rhs_sep0 = gaussian(streams_of[7], (S, R), 1.0, 6.0, ((0, 512),), jnp.float32)
    inv_sep0 = draw_inv_sep0(jax.random.fold_in(streams_of[9], 71), 0)
    return {"rhs_local": rhs_local, "inv_local": inv_local, "couple_local": couple_local, "row_index": row_index, "rhs_sep1": rhs_sep1, "inv_sep1": inv_sep1, "couple_sep1": couple_sep1, "rhs_sep0": rhs_sep0, "inv_sep0": inv_sep0}


def reference(rhs_local, inv_local, couple_local, row_index, rhs_sep1, inv_sep1, couple_sep1, rhs_sep0, inv_sep0):
    highest = lax.Precision.HIGHEST
    units = N_LEAF * N_BLK
    inv_blocks = inv_local.reshape(units, SD, SD)
    rhs_blocks = rhs_local.reshape(units, SD, R)
    couple_blocks = couple_local.reshape(units, SD, K)

    def forward_one(items):
        inv_one, rhs_one, couple_one = items
        solved = jnp.dot(inv_one, rhs_one, precision=highest, preferred_element_type=jnp.float32)
        lifted = jnp.dot(couple_one.T, solved, precision=highest, preferred_element_type=jnp.float32)
        return solved, lifted

    solved_local, lifted = lax.map(forward_one, (inv_blocks, rhs_blocks, couple_blocks))
    device = jnp.arange(units, dtype=jnp.int32)
    level_one = (device // (units // 2))[:, None]
    target = jnp.where(row_index < S, level_one * S + row_index, 2 * S + row_index - S).astype(jnp.int32)
    update = jax.ops.segment_sum(lifted.reshape(units * K, R), target.reshape(-1), num_segments=3 * S)
    update_one = update[:2 * S].reshape(2, S, R)
    update_root = update[2 * S:]
    inv_one = inv_sep1.reshape(2, S, S)
    couple_one = couple_sep1.reshape(2, S, S)
    solved_one = jnp.einsum('jik,jkr->jir', inv_one, rhs_sep1.reshape(2, S, R) - update_one, precision=highest)
    update_root = update_root + jnp.einsum('jik,jir->kr', couple_one, solved_one, precision=highest)
    solved_root = jnp.dot(inv_sep0, rhs_sep0 - update_root, precision=highest, preferred_element_type=jnp.float32)
    x_root = jnp.dot(inv_sep0.T, solved_root, precision=highest, preferred_element_type=jnp.float32)
    rest_one = solved_one - jnp.einsum('jik,kr->jir', couple_one, x_root, precision=highest)
    x_one = jnp.einsum('jki,jkr->jir', inv_one, rest_one, precision=highest)
    stacked = jnp.concatenate([x_one.reshape(2 * S, R), x_root], axis=0)
    gathered = stacked[target]

    def backward_one(items):
        inv_block, solved, couple_block, above = items
        rest = solved - jnp.dot(couple_block, above, precision=highest, preferred_element_type=jnp.float32)
        return jnp.dot(inv_block.T, rest, precision=highest, preferred_element_type=jnp.float32)

    x_local = lax.map(backward_one, (inv_blocks, solved_local, couple_blocks, gathered))
    return (x_local.reshape(units * SD, R), x_one.reshape(2 * S, R), x_root)
```

```python
import jax
import jax.numpy as jnp
from jax import lax
from jax.sharding import Mesh
from jax.sharding import PartitionSpec as P

HIGHEST = lax.Precision.HIGHEST
PLANE = ("core", "blk")
HALF = ("plane",)
LINE = ("half", "plane")


def product(left, right, left_dim, right_dim):
    dims = (((left_dim,), (right_dim,)), ((), ()))
    return lax.dot_general(left, right, dims, precision=HIGHEST, preferred_element_type=jnp.float32)


def exchange(slots, axes):
    return lax.all_to_all(slots, axes, 0, 0)


def spread(value, axes):
    return exchange(jnp.broadcast_to(value[None], (lax.axis_size(axes),) + value.shape), axes)


def total(value, axes):
    return jnp.sum(spread(value, axes), axis=0)


def by_member(wide, members):
    rows, columns = wide.shape
    return wide.reshape(rows, members, columns // members).transpose(1, 0, 2)


def side_by_side(stacked):
    members, rows, columns = stacked.shape
    return stacked.transpose(1, 0, 2).reshape(rows, members * columns)


def place_rows(values, own_rows, offset):
    current = lax.dynamic_slice_in_dim(values, offset, own_rows.shape[0], 0)
    return lax.dynamic_update_slice_in_dim(values, current + own_rows, offset, 0)


def shards(
    rhs_local,
    inv_local,
    couple_local,
    row_index,
    rhs_sep1,
    inv_sep1,
    couple_sep1,
    rhs_sep0,
    inv_sep0,
):
    sep_rows = inv_sep0.shape[1]
    samples = rhs_local.shape[1]
    rows_one = rhs_sep1.shape[0]
    rows_root = rhs_sep0.shape[0]
    members = lax.axis_size(PLANE)
    flat_index = lax.axis_index(("half", "plane", "core", "blk"))
    all_devices = lax.axis_size(("half", "plane", "core", "blk"))
    offset_one = flat_index % (all_devices // 2) * rows_one
    offset_root = flat_index * rows_root

    solved_local = product(rhs_local, inv_local, 0, 1)
    lifted = product(couple_local, solved_local, 0, 1)
    negated = jnp.zeros((2 * sep_rows, samples), jnp.float32).at[row_index[0]].add(-lifted)
    negated = place_rows(negated, rhs_sep1, offset_one)
    negated = place_rows(negated, rhs_sep0, sep_rows + offset_root)
    negated = negated.T

    slots = jnp.concatenate(
        [by_member(negated[:, :sep_rows], members), by_member(inv_sep1, members), by_member(inv_sep0, members)],
        axis=1,
    )
    slots = exchange(slots, PLANE)
    columns = slots.shape[2]
    inv_one = slots[:, samples : samples + rows_one].reshape(members * rows_one, columns)
    inv_root = slots[:, samples + rows_one :].reshape(members * rows_root, columns)

    right_one = total(jnp.sum(slots[:, :samples], axis=0), HALF)
    solved_one = product(inv_one, right_one, 1, 1)
    solved_one = jnp.sum(exchange(solved_one.reshape(members, rows_one, samples), PLANE), axis=0)

    right_root = negated[:, sep_rows:] - product(solved_one, couple_sep1, 0, 0)
    right_root = jnp.sum(exchange(by_member(right_root, members), PLANE), axis=0)
    right_root = total(right_root, LINE)
    solved_root = total(product(right_root, inv_root, 1, 1), PLANE)
    x_root = total(product(solved_root, inv_root, 1, 0), LINE)
    x_root = side_by_side(spread(x_root, PLANE))

    rest_one = solved_one - product(couple_sep1, x_root, 1, 1)
    rest_one = spread(rest_one, PLANE).reshape(members * rows_one, samples)
    x_one = total(product(rest_one, inv_one, 0, 0), HALF)
    x_one = side_by_side(spread(x_one, PLANE))

    ancestor = jnp.concatenate([x_one, x_root], axis=1).T
    rest_local = solved_local - product(ancestor[row_index[0]], couple_local, 0, 1)
    x_local = product(inv_local, rest_local, 0, 1)
    own_one = lax.dynamic_slice_in_dim(ancestor, offset_one, rows_one, 0)
    own_root = lax.dynamic_slice_in_dim(ancestor, sep_rows + offset_root, rows_root, 0)
    return (x_local, own_one, own_root)


def solution(mesh):
    leaf, blk = mesh.devices.shape
    halves = Mesh(mesh.devices.reshape(2, leaf // 4, 2, blk), ("half", "plane", "core", "blk"))
    spec = P(("half", "plane", "core", "blk"), None)
    return jax.shard_map(shards, mesh=halves, in_specs=(spec,) * 9, out_specs=(spec,) * 3, check_vma=False)
```

```python
import functools

import jax
import jax.numpy as jnp
from jax import lax
from jax.experimental import pallas as pl
from jax.experimental.pallas import tpu as pltpu
from jax.sharding import Mesh
from jax.sharding import PartitionSpec as P

PLANE = ("core", "blk")
HALF = ("plane",)
LINE = ("half", "plane")
EVERY = ("half", "plane", "core", "blk")

VMEM = pl.BlockSpec(memory_space=pltpu.VMEM)
SMEM = pl.BlockSpec(memory_space=pltpu.SMEM)
HBM = pl.BlockSpec(memory_space=pltpu.HBM)
LANES = 128
UNROLL = 16


def halves(value):
    high = value.astype(jnp.bfloat16)
    return high, (value - high.astype(jnp.float32)).astype(jnp.bfloat16)


def dot16(left, right):
    return jnp.dot(left, right, preferred_element_type=jnp.float32)


def tall_product(left, right):
    n = right.shape[1]
    left_high, left_low = halves(left)
    right_high, right_low = halves(right)
    both = dot16(left_high, jnp.concatenate([right_high, right_low], axis=1))
    return both[:, :n] + (both[:, n:] + dot16(left_low, right_high))


def wide_product(left, right):
    m = left.shape[0]
    left_high, left_low = halves(left)
    right_high, right_low = halves(right)
    both = dot16(jnp.concatenate([left_high, left_low], axis=0), right_high)
    return both[:m] + (both[m:] + dot16(left_high, right_low))


def fetch(pairs, sems):
    copies = [pltpu.make_async_copy(source, target, sems.at[k]) for k, (source, target) in enumerate(pairs)]
    for copy in copies:
        copy.start()
    return copies


def own_position(axes):
    position = lax.axis_index(axes[0])
    for axis in axes[1:]:
        position = position * lax.axis_size(axis) + lax.axis_index(axis)
    return position


def forward_kernel(
    position, rhs, inv, couple, index, rhs_one, inv_one, rhs_root, inv_root, slots, root, solved,
    rhs_here, inv_here, couple_here, index_here, rhs_one_here, inv_one_here, rhs_root_here, inv_root_here, update, lifted, sems,
):
    copies = fetch(
        [
            (rhs, rhs_here),
            (inv, inv_here),
            (index, index_here),
            (couple, couple_here),
            (rhs_one, rhs_one_here),
            (rhs_root, rhs_root_here),
            (inv_one, inv_one_here),
            (inv_root, inv_root_here),
        ],
        sems,
    )
    get_rhs, get_inv, get_index, get_couple, get_rhs_one, get_rhs_root, get_inv_one, get_inv_root = copies
    samples = rhs.shape[0]
    count = index.shape[1]
    rows_one = rhs_one.shape[0]
    rows_root = rhs_root.shape[0]
    sep_rows = inv_one.shape[1]
    members = slots.shape[0]

    @pl.loop(0, update.shape[0] // 512)
    def _(step):
        update[pl.ds(pl.multiple_of(step * 512, 512), 512), :] = jnp.zeros((512, samples), jnp.float32)

    get_rhs.wait()
    get_inv.wait()
    y = tall_product(inv_here[...], rhs_here[...].T)
    solved[...] = y
    y = -y.T
    get_couple.wait()
    step = couple_here.shape[1] // 2
    for start in range(0, couple_here.shape[1], step):
        lifted[start : start + step, :] = wide_product(y, couple_here[:, start : start + step]).T

    get_index.wait()

    @pl.loop(0, count // UNROLL)
    def _(step):
        base = pl.multiple_of(step * UNROLL, UNROLL)
        for k in range(UNROLL):
            update[pl.ds(index_here[0, base + k], 1), :] = lifted[pl.ds(base + k, 1), :]

    get_rhs_one.wait()
    get_rhs_root.wait()
    here = position()
    own_one = pl.ds(pl.multiple_of(here % (sep_rows // rows_one) * rows_one, rows_one), rows_one)
    update[own_one, :] = update[own_one, :] + rhs_one_here[...]
    own_root = pl.ds(pl.multiple_of(sep_rows + here * rows_root, rows_root), rows_root)
    update[own_root, :] = update[own_root, :] + rhs_root_here[...]

    group = LANES // samples
    for first in range(0, 2 * members, group):
        packed = jnp.concatenate([update[(first + g) * LANES : (first + g + 1) * LANES, :] for g in range(group)], axis=1).T
        for g in range(group):
            piece = packed[g * samples : (g + 1) * samples]
            if first < members:
                slots[first + g, :samples, :] = piece
            else:
                root[first + g - members] = piece

    get_inv_one.wait()
    get_inv_root.wait()
    for member in range(members):
        columns = slice(member * LANES, (member + 1) * LANES)
        slots[member, samples : samples + rows_one, :] = inv_one_here[:, columns]
        slots[member, samples + rows_one :, :] = inv_root_here[:, columns]


def forward(rhs_local, inv_local, couple_local, row_index, rhs_sep1, inv_sep1, rhs_sep0, inv_sep0, position):
    samples = rhs_local.shape[1]
    members = inv_sep1.shape[1] // LANES
    slot_rows = samples + inv_sep1.shape[0] + inv_sep0.shape[0]
    given = (rhs_local.T, inv_local, couple_local, row_index, rhs_sep1, inv_sep1, rhs_sep0, inv_sep0)
    here = [pltpu.VMEM(array.shape, array.dtype) for array in given]
    here[3] = pltpu.SMEM(row_index.shape, row_index.dtype)
    return pl.pallas_call(
        functools.partial(forward_kernel, position),
        out_shape=(
            jax.ShapeDtypeStruct((members, slot_rows, LANES), jnp.float32),
            jax.ShapeDtypeStruct((members, samples, LANES), jnp.float32),
            jax.ShapeDtypeStruct(rhs_local.shape, jnp.float32),
        ),
        in_specs=[HBM] * len(given),
        out_specs=(VMEM, VMEM, VMEM),
        scratch_shapes=here
        + [
            pltpu.VMEM((2 * inv_sep1.shape[1], samples), jnp.float32),
            pltpu.VMEM((couple_local.shape[1], samples), jnp.float32),
            pltpu.SemaphoreType.DMA((len(given),)),
        ],
        compiler_params=pltpu.CompilerParams(vmem_limit_bytes=63 * 2**20),
        name="local_forward",
    )(*given)


def backward_kernel(
    position, one, root, solved, inv, couple, index, x_local, own_one, own_root,
    inv_here, couple_here, index_here, ancestor, above, sems,
):
    get_index, get_couple, get_inv = fetch([(index, index_here), (couple, couple_here), (inv, inv_here)], sems)
    samples = solved.shape[1]
    count = index.shape[1]
    members = one.shape[0]
    sep_rows = members * LANES
    group = LANES // samples
    for first in range(0, 2 * members, group):
        source = one if first < members else root
        start = first % members
        packed = source[start : start + group].reshape(LANES, LANES).T
        for g in range(group):
            ancestor[(first + g) * LANES : (first + g + 1) * LANES, :] = packed[:, g * samples : (g + 1) * samples]

    here = position()
    rows_one = own_one.shape[0]
    rows_root = own_root.shape[0]
    own_one[...] = ancestor[pl.ds(pl.multiple_of(here % (sep_rows // rows_one) * rows_one, rows_one), rows_one), :]
    own_root[...] = ancestor[pl.ds(pl.multiple_of(sep_rows + here * rows_root, rows_root), rows_root), :]
    get_index.wait()

    @pl.loop(0, count // UNROLL)
    def _(step):
        base = pl.multiple_of(step * UNROLL, UNROLL)
        for k in range(UNROLL):
            above[pl.ds(base + k, 1), :] = ancestor[pl.ds(index_here[0, base + k], 1), :]

    get_couple.wait()
    rest = solved[...] - tall_product(couple_here[...], above[...])
    get_inv.wait()
    x_local[...] = wide_product(rest.T, inv_here[...])


def backward(one, root, solved, inv_local, couple_local, row_index, rows_one, rows_root, position):
    samples = solved.shape[1]
    x_local, own_one, own_root = pl.pallas_call(
        functools.partial(backward_kernel, position),
        out_shape=(
            jax.ShapeDtypeStruct(solved.shape[::-1], jnp.float32),
            jax.ShapeDtypeStruct((rows_one, samples), jnp.float32),
            jax.ShapeDtypeStruct((rows_root, samples), jnp.float32),
        ),
        in_specs=[VMEM, VMEM, VMEM, HBM, HBM, HBM],
        out_specs=(VMEM, VMEM, VMEM),
        scratch_shapes=[
            pltpu.VMEM(inv_local.shape, jnp.float32),
            pltpu.VMEM(couple_local.shape, jnp.float32),
            pltpu.SMEM(row_index.shape, row_index.dtype),
            pltpu.VMEM((2 * one.shape[0] * LANES, samples), jnp.float32),
            pltpu.VMEM((couple_local.shape[1], samples), jnp.float32),
            pltpu.SemaphoreType.DMA((3,)),
        ],
        compiler_params=pltpu.CompilerParams(vmem_limit_bytes=63 * 2**20),
        name="local_backward",
    )(one, root, solved, inv_local, couple_local, row_index)
    return x_local.T, own_one, own_root


def own_index():
    return own_position(EVERY)


def kernel_call(body, out_shapes, name):
    return pl.pallas_call(
        body,
        out_shape=tuple(jax.ShapeDtypeStruct(shape, jnp.float32) for shape in out_shapes),
        compiler_params=pltpu.CompilerParams(vmem_limit_bytes=16 * 2**20),
        name=name,
    )


def summed(parts):
    count = parts.shape[0]
    terms = [parts[k] for k in range(count)]
    while len(terms) > 1:
        terms = [a + b for a, b in zip(terms[::2], terms[1::2], strict=True)]
    return terms[0]


def pair_rows(stacked, rows, which):
    piece = stacked[:, rows + 8 * which : rows + 8 * which + 8, :]
    return piece.reshape(piece.shape[0] * 8, LANES)


def solve_one_kernel(parts, slots, out):
    samples = parts.shape[1]
    members = out.shape[0]
    right = summed(parts).T
    solved = [tall_product(pair_rows(slots, samples, g), right) for g in range(2)]
    blank = jnp.zeros((members * 8, LANES - 2 * samples), jnp.float32)
    out[...] = jnp.concatenate([*solved, blank], axis=1).reshape(members, 8, LANES)


def couple_up_kernel(parts, root, couple, out, solved):
    samples = root.shape[1]
    total_here = summed(parts)
    solved[...] = total_here
    flipped = total_here.T
    y = jnp.concatenate([flipped[:samples], flipped[samples : 2 * samples]], axis=1)
    lifted = wide_product(y, couple[...])
    for member in range(out.shape[0]):
        out[member] = root[member] - lifted[:, member * LANES : (member + 1) * LANES]


def solve_root_kernel(parts, slots, out):
    samples = parts.shape[1]
    members, rows, _ = out.shape
    first = slots.shape[1] - 8
    right = summed(parts).T
    y = tall_product(slots[:, first:, :].reshape(members * 8, LANES), right)
    y = jnp.concatenate([y[g * rows : (g + 1) * rows] for g in range(LANES // samples)], axis=1)
    for member in range(members):
        out[member] = y


def lift_root_kernel(parts, slots, out):
    members, rows, _ = parts.shape
    samples = out.shape[1]
    first = slots.shape[1] - 8
    flipped = summed(parts).T
    y = jnp.concatenate([flipped[g * samples : (g + 1) * samples] for g in range(LANES // samples)], axis=1)
    x = wide_product(y, slots[:, first:, :].reshape(members * 8, LANES))
    for member in range(out.shape[0]):
        out[member] = x


def rest_one_kernel(root, solved, couple, out):
    members, samples, _ = root.shape
    flat = jnp.concatenate([root[member] for member in range(members)], axis=1)
    flat = jnp.concatenate(halves(flat), axis=0)
    rows = couple.shape[0]
    both = jnp.concatenate(halves(couple[...]), axis=0)
    dims = (((1,), (1,)), ((), ()))
    every = lax.dot_general(both, flat, dims, preferred_element_type=jnp.float32)
    down = every[:rows, :samples] + (every[:rows, samples:] + every[rows:, :samples])
    blank = jnp.zeros((8, LANES - 2 * samples), jnp.float32)
    rest = solved[...] - jnp.concatenate([down[:8], down[8:], blank], axis=1)
    for member in range(members):
        out[member] = rest


def lift_one_kernel(parts, slots, out):
    members = parts.shape[0]
    samples = out.shape[1]
    flipped = parts[...].reshape(members * 8, LANES).T
    x = [wide_product(flipped[g * samples : (g + 1) * samples], pair_rows(slots, samples, g)) for g in range(2)]
    x = x[0] + x[1]
    for member in range(out.shape[0]):
        out[member] = x


def exchange(slots, axes):
    return lax.all_to_all(slots, axes, 0, 0)


def spread(value, axes):
    return exchange(jnp.broadcast_to(value[None], (lax.axis_size(axes),) + value.shape), axes)


def shards(
    rhs_local,
    inv_local,
    couple_local,
    row_index,
    rhs_sep1,
    inv_sep1,
    couple_sep1,
    rhs_sep0,
    inv_sep0,
):
    samples = rhs_local.shape[1]
    members = lax.axis_size(PLANE)
    piece = (samples, LANES)

    slots, root, solved_local = forward(
        rhs_local, inv_local, couple_local, row_index, rhs_sep1, inv_sep1, rhs_sep0, inv_sep0, own_index
    )
    slots = exchange(slots, PLANE)
    parts = spread(jnp.sum(slots[:, :samples], axis=0), HALF)
    (parts,) = kernel_call(solve_one_kernel, [(members, 8, LANES)], "solve_one")(parts, slots)
    parts, solved_one = kernel_call(couple_up_kernel, [(members, *piece), (8, LANES)], "couple_up")(
        exchange(parts, PLANE), root, couple_sep1
    )
    parts = spread(jnp.sum(exchange(parts, PLANE), axis=0), LINE)
    rows = members * rhs_sep0.shape[0] * samples // LANES
    (parts,) = kernel_call(solve_root_kernel, [(members, rows, LANES)], "solve_root")(parts, slots)
    (parts,) = kernel_call(lift_root_kernel, [(lax.axis_size(LINE), *piece)], "lift_root")(exchange(parts, PLANE), slots)
    x_root = spread(jnp.sum(exchange(parts, LINE), axis=0), PLANE)
    (parts,) = kernel_call(rest_one_kernel, [(members, 8, LANES)], "rest_one")(x_root, solved_one, couple_sep1)
    (parts,) = kernel_call(lift_one_kernel, [(lax.axis_size(HALF), *piece)], "lift_one")(exchange(parts, PLANE), slots)
    x_one = spread(jnp.sum(exchange(parts, HALF), axis=0), PLANE)
    return backward(
        x_one, x_root, solved_local, inv_local, couple_local, row_index, rhs_sep1.shape[0], rhs_sep0.shape[0], own_index
    )


def solution(mesh):
    leaf, blk = mesh.devices.shape
    halves_mesh = Mesh(mesh.devices.reshape(2, leaf // 4, 2, blk), EVERY)
    spec = P(EVERY, None)
    return jax.shard_map(shards, mesh=halves_mesh, in_specs=(spec,) * 9, out_specs=(spec,) * 3, check_vma=False)
```

```python
import functools

import jax
import jax.numpy as jnp
from jax import lax
from jax.experimental import pallas as pl
from jax.experimental.pallas import tpu as pltpu
from jax.sharding import Mesh
from jax.sharding import PartitionSpec as P

GROUP = ("near", "core", "blk")
HALF = ("pair",)
LINE = ("half", "pair")
EVERY = LINE + GROUP

VMEM = pl.BlockSpec(memory_space=pltpu.VMEM)
SMEM = pl.BlockSpec(memory_space=pltpu.SMEM)
HBM = pl.BlockSpec(memory_space=pltpu.HBM)
LANES = 128
UNROLL = 32


def halves(value):
    high = value.astype(jnp.bfloat16)
    return high, (value - high.astype(jnp.float32)).astype(jnp.bfloat16)


def dot16(left, right):
    return jnp.dot(left, right, preferred_element_type=jnp.float32)


def tall_product(left, right):
    n = right.shape[1]
    left_high, left_low = halves(left)
    right_high, right_low = halves(right)
    both = dot16(left_high, jnp.concatenate([right_high, right_low], axis=1))
    return both[:, :n] + (both[:, n:] + dot16(left_low, right_high))


def wide_product(left, right):
    m = left.shape[0]
    left_high, left_low = halves(left)
    right_high, right_low = halves(right)
    both = dot16(jnp.concatenate([left_high, left_low], axis=0), right_high)
    return both[:m] + (both[m:] + dot16(left_high, right_low))


PILES = 4


def lane_piles(rows):
    return lax.broadcasted_iota(jnp.int32, (rows, LANES), 1) // (LANES // PILES)


def deal(stacks, width):
    granule = lax.broadcasted_iota(jnp.int32, stacks[0].shape, 1) // width
    turned = [stack if k == 0 else pltpu.roll(stack, width * k, 1) for k, stack in enumerate(stacks)]
    count = LANES // width
    for first in range(count):
        row = jnp.zeros_like(stacks[0])
        for k, stack in enumerate(turned):
            row = jnp.where(granule == (first + k) % count, stack, row)
        yield row if first == 0 else pltpu.roll(row, LANES - width * first, 1)


def fetch(pairs, sems):
    copies = [pltpu.make_async_copy(source, target, sems.at[k]) for k, (source, target) in enumerate(pairs)]
    for copy in copies:
        copy.start()
    return copies


def own_position(axes):
    position = lax.axis_index(axes[0])
    for axis in axes[1:]:
        position = position * lax.axis_size(axis) + lax.axis_index(axis)
    return position


def forward_kernel(
    position, rhs, inv, couple, index, rhs_one, inv_one, rhs_root, inv_root, slots, inv_slots, root, solved,
    rhs_here, inv_here, couple_here, index_here, rhs_one_here, inv_one_here, rhs_root_here, inv_root_here, update, lifted, sems,
):
    copies = fetch(
        [
            (inv_one, inv_one_here),
            (inv_root, inv_root_here),
            (rhs, rhs_here),
            (inv, inv_here),
            (index, index_here),
            (couple, couple_here),
            (rhs_one, rhs_one_here),
            (rhs_root, rhs_root_here),
        ],
        sems,
    )
    get_inv_one, get_inv_root, get_rhs, get_inv, get_index, get_couple, get_rhs_one, get_rhs_root = copies
    count = index.shape[1]
    rows_one = rhs_one.shape[0]
    rows_root = rhs_root.shape[0]
    sep_rows = inv_one.shape[1]
    pile = sep_rows // PILES
    depth = root.shape[1]

    @pl.loop(0, 2 * sep_rows // 512)
    def _(step):
        update[pl.ds(pl.multiple_of(step * 512, 512), 512), :] = jnp.zeros((512, LANES), jnp.float32)

    get_inv_one.wait()
    get_inv_root.wait()
    for first in range(0, pile, LANES):
        columns = [slice(g * pile + first, g * pile + first + LANES) for g in range(PILES)]
        stacks = [inv_one_here[r : r + rows_one // 2, c] for r in (0, rows_one // 2) for c in columns]
        for k, row in enumerate(deal(stacks, depth)):
            slots[first // depth + k, depth:, :] = row
        stacks = [inv_root_here[r : r + rows_root // 2, c] for r in (0, rows_root // 2) for c in columns]
        for k, row in enumerate(deal(stacks, depth)):
            inv_slots[first // depth + k, rows_root // 2 :, :] = row

    get_rhs.wait()
    get_inv.wait()
    y = tall_product(inv_here[...], rhs_here[...].T)
    solved[...] = y
    y = -y.T
    get_index.wait()
    get_couple.wait()
    step = couple_here.shape[1] // 2
    for start in range(0, couple_here.shape[1], step):
        part = wide_product(y, couple_here[:, start : start + step])
        lifted[start : start + step, :] = jnp.concatenate([part] * PILES, axis=0).T

    @pl.loop(0, count // UNROLL)
    def _(step):
        base = pl.multiple_of(step * UNROLL, UNROLL)
        for k in range(UNROLL):
            update[pl.ds(index_here[0, base + k], 1), :] = lifted[pl.ds(base + k, 1), :]

    get_rhs_one.wait()
    get_rhs_root.wait()
    here = position()
    own_one = pl.ds(pl.multiple_of(here % (sep_rows // rows_one) * rows_one, rows_one), rows_one)
    update[own_one, :] = update[own_one, :] + jnp.concatenate([rhs_one_here[...]] * PILES, axis=1)
    own_root = pl.ds(pl.multiple_of(sep_rows + here * rows_root, rows_root), rows_root)
    update[own_root, :] = update[own_root, :] + jnp.concatenate([rhs_root_here[...]] * PILES, axis=1)

    piles = lane_piles(depth)
    for base in (0, sep_rows):
        for member in range(root.shape[0]):
            rows = [update[base + g * pile + member * depth : base + g * pile + (member + 1) * depth, :] for g in range(PILES)]
            piece = rows[0]
            for g in range(1, PILES):
                piece = jnp.where(piles == g, rows[g], piece)
            if base == 0:
                slots[member, :depth, :] = piece
            else:
                root[member] = piece


def forward(rhs_local, inv_local, couple_local, row_index, rhs_sep1, inv_sep1, rhs_sep0, inv_sep0, position):
    samples = rhs_local.shape[1]
    members = lax.axis_size(GROUP)
    depth = inv_sep1.shape[1] // members // PILES
    slot_rows = depth + inv_sep1.shape[0] // 2
    given = (rhs_local.T, inv_local, couple_local, row_index, rhs_sep1, inv_sep1, rhs_sep0, inv_sep0)
    here = [pltpu.VMEM(array.shape, array.dtype) for array in given]
    here[3] = pltpu.SMEM(row_index.shape, row_index.dtype)
    return pl.pallas_call(
        functools.partial(forward_kernel, position),
        out_shape=(
            jax.ShapeDtypeStruct((members, slot_rows, LANES), jnp.float32),
            jax.ShapeDtypeStruct((members, inv_sep0.shape[0], LANES), jnp.float32),
            jax.ShapeDtypeStruct((members, depth, LANES), jnp.float32),
            jax.ShapeDtypeStruct(rhs_local.shape, jnp.float32),
        ),
        in_specs=[HBM] * len(given),
        out_specs=(VMEM, VMEM, VMEM, VMEM),
        scratch_shapes=here
        + [
            pltpu.VMEM((2 * inv_sep1.shape[1], LANES), jnp.float32),
            pltpu.VMEM((couple_local.shape[1], LANES), jnp.float32),
            pltpu.SemaphoreType.DMA((len(given),)),
        ],
        compiler_params=pltpu.CompilerParams(vmem_limit_bytes=63 * 2**20),
        name="local_forward",
    )(*given)


def backward_kernel(
    position, one, root, solved, inv, couple, index, x_local, own_one, own_root,
    inv_here, couple_here, index_here, ancestor, above, sems,
):
    get_index, get_couple, get_inv = fetch([(index, index_here), (couple, couple_here), (inv, inv_here)], sems)
    samples = solved.shape[1]
    count = index.shape[1]
    members, depth, _ = one.shape
    pile = members * depth
    sep_rows = PILES * pile
    piles = lane_piles(LANES)
    step = LANES // depth
    for base, source in ((0, one), (sep_rows, root)):
        for member in range(0, members, step):
            rows = source[member : member + step].reshape(LANES, LANES)
            for g in range(PILES):
                start = base + g * pile + member * depth
                ancestor[start : start + LANES, :] = jnp.where(piles == g, rows, 0.0)
    here = position()

    def take_own(start, out):
        wide = ancestor[pl.ds(pl.multiple_of(start, out.shape[0]), out.shape[0]), :]
        taken = wide[:, :samples]
        for g in range(1, PILES):
            taken = taken + wide[:, g * samples : (g + 1) * samples]
        out[...] = taken

    take_own(here % (sep_rows // own_one.shape[0]) * own_one.shape[0], own_one)
    take_own(sep_rows + here * own_root.shape[0], own_root)
    get_index.wait()

    @pl.loop(0, count // UNROLL)
    def _(step):
        base = pl.multiple_of(step * UNROLL, UNROLL)
        for k in range(UNROLL):
            above[pl.ds(base + k, 1), :] = ancestor[pl.ds(index_here[0, base + k], 1), :]

    get_couple.wait()
    down = tall_product(couple_here[...], above[...])
    rest = solved[...]
    for g in range(PILES):
        rest = rest - down[:, g * samples : (g + 1) * samples]
    get_inv.wait()
    x_local[...] = wide_product(rest.T, inv_here[...])


def backward(one, root, solved, inv_local, couple_local, row_index, rows_one, rows_root, position):
    samples = solved.shape[1]
    x_local, own_one, own_root = pl.pallas_call(
        functools.partial(backward_kernel, position),
        out_shape=(
            jax.ShapeDtypeStruct(solved.shape[::-1], jnp.float32),
            jax.ShapeDtypeStruct((rows_one, samples), jnp.float32),
            jax.ShapeDtypeStruct((rows_root, samples), jnp.float32),
        ),
        in_specs=[VMEM, VMEM, VMEM, HBM, HBM, HBM],
        out_specs=(VMEM, VMEM, VMEM),
        scratch_shapes=[
            pltpu.VMEM(inv_local.shape, jnp.float32),
            pltpu.VMEM(couple_local.shape, jnp.float32),
            pltpu.SMEM(row_index.shape, row_index.dtype),
            pltpu.VMEM((2 * PILES * one.shape[0] * one.shape[1], LANES), jnp.float32),
            pltpu.VMEM((couple_local.shape[1], LANES), jnp.float32),
            pltpu.SemaphoreType.DMA((3,)),
        ],
        compiler_params=pltpu.CompilerParams(vmem_limit_bytes=63 * 2**20),
        name="local_backward",
    )(one, root, solved, inv_local, couple_local, row_index)
    return x_local.T, own_one, own_root


def own_index():
    return own_position(EVERY)


def kernel_call(body, out_shapes, name, scratch=()):
    return pl.pallas_call(
        body,
        out_shape=tuple(jax.ShapeDtypeStruct(shape, jnp.float32) for shape in out_shapes),
        scratch_shapes=[pltpu.VMEM(shape, jnp.float32) for shape in scratch],
        compiler_params=pltpu.CompilerParams(vmem_limit_bytes=16 * 2**20),
        name=name,
    )


def summed(parts):
    terms = [parts[k] for k in range(parts.shape[0])]
    while len(terms) > 1:
        terms = [a + b for a, b in zip(terms[::2], terms[1::2], strict=True)]
    return terms[0]


def rows_of(piece):
    samples = LANES // PILES
    return jnp.concatenate([piece[:, g * samples : (g + 1) * samples] for g in range(PILES)], axis=0)


def piece_of(rows):
    depth = rows.shape[0] // PILES
    return jnp.concatenate([rows[g * depth : (g + 1) * depth] for g in range(PILES)], axis=1)


def inv_one_block(slots):
    piece = slots[:, slots.shape[1] - 8 :, :]
    return piece.reshape(piece.shape[0] * 8, LANES)


def inv_root_block(mixed):
    members = mixed.shape[0] // 8
    return jnp.concatenate([mixed[pl.ds(4 + i, members, stride=8), :] for i in range(4)], axis=0)


def twice(rows):
    blank = jnp.zeros_like(rows)
    return jnp.concatenate(
        [jnp.concatenate([rows, blank], axis=1), jnp.concatenate([blank, rows], axis=1)],
        axis=0,
    )


def solve_one_kernel(parts, slots, inv_slots, out, scratch):
    scratch[...] = tall_product(inv_one_block(slots), twice(rows_of(summed(parts))))
    members = scratch.shape[0] // 8
    out[...] = inv_slots[...]
    for i in range(4):
        pieces = [scratch[pl.ds(4 * h + i, members, stride=8), :] for h in range(2)]
        out[pl.ds(i, members, stride=8), :] = jnp.concatenate(pieces, axis=1)


def couple_up_kernel(parts, root, couple, out, solved):
    samples = LANES // PILES
    total_here = summed(parts)[: solved.shape[0]]
    solved[...] = total_here
    flipped = total_here.T
    order = [(g, h) for g in range(2) for h in range(2)]
    y = jnp.concatenate([flipped[(2 * h + g) * samples : (2 * h + g + 1) * samples] for g, h in order], axis=1)
    lifted = wide_product(y, couple[...])
    pile = lifted.shape[1] // PILES
    lifted = jnp.concatenate([lifted[:, g * pile : (g + 1) * pile] for g in range(PILES)], axis=0).T
    out[...] = root[...] - lifted.reshape(root.shape)


def solve_root_kernel(parts, mixed, out):
    y = tall_product(inv_root_block(mixed), twice(rows_of(summed(parts))))
    rows = out.shape[0]
    out[...] = jnp.concatenate([y[:rows], y[rows:]], axis=1)


def lift_root_kernel(solved, mixed, out):
    half = LANES // 2
    samples = LANES // PILES
    flipped = solved[...].T
    y = jnp.concatenate([flipped[:half], flipped[half:]], axis=1)
    every = wide_product(y, inv_root_block(mixed))
    piece = piece_of((every[:samples, :half] + every[samples:, half:]).T)
    for member in range(out.shape[0]):
        out[member] = piece


def rest_one_kernel(root, solved, couple, out):
    samples = LANES // PILES
    rows, columns = couple.shape
    pile = columns // PILES
    stacked = jnp.concatenate([couple[:, g * pile : (g + 1) * pile] for g in range(PILES)], axis=0)
    every = wide_product(stacked, root[...].reshape(pile, LANES))
    down = every[:rows, :samples]
    for g in range(1, PILES):
        down = down + every[g * rows : (g + 1) * rows, g * samples : (g + 1) * samples]
    order = [(h, g) for h in range(2) for g in range(2)]
    out[...] = solved[...] - jnp.concatenate([down[8 * g + 4 * h : 8 * g + 4 * h + 4] for h, g in order], axis=1)


def lift_one_kernel(rest, slots, out, scratch):
    samples = LANES // PILES
    members = rest.shape[0] // 4
    for i in range(4):
        pieces = rest[pl.ds(i, members, stride=4), :]
        for h in range(2):
            scratch[pl.ds(4 * h + i, members, stride=8), :] = pieces[:, 2 * samples * h : 2 * samples * (h + 1)]
    every = wide_product(scratch[...].T, inv_one_block(slots))
    half = LANES // 2
    piece = piece_of((every[:samples, :half] + every[samples:, half:]).T)
    for member in range(out.shape[0]):
        out[member] = piece


def exchange(slots, axes):
    return lax.all_to_all(slots, axes, 0, 0)


def spread(value, axes):
    return exchange(jnp.broadcast_to(value[None], (lax.axis_size(axes),) + value.shape), axes)


def shards(
    rhs_local,
    inv_local,
    couple_local,
    row_index,
    rhs_sep1,
    inv_sep1,
    couple_sep1,
    rhs_sep0,
    inv_sep0,
):
    samples = rhs_local.shape[1]
    members = lax.axis_size(GROUP)
    rows_one, rows_root = rhs_sep1.shape[0], rhs_sep0.shape[0]
    piece = (inv_sep0.shape[1] // members // PILES, LANES)
    block_one = (members * rows_one * samples // LANES, LANES)
    block_root = (members * rows_root * samples // LANES, LANES)
    flat_one = (members * rows_one // 2, 2 * samples)

    slots, inv_slots, root, solved_local = forward(
        rhs_local, inv_local, couple_local, row_index, rhs_sep1, inv_sep1, rhs_sep0, inv_sep0, own_index
    )
    slots = exchange(slots, GROUP)
    parts = spread(jnp.sum(slots[:, : piece[0]], axis=0), HALF)
    mixed = (members * inv_slots.shape[1], LANES)
    (parts,) = kernel_call(solve_one_kernel, [mixed], "solve_one", [flat_one])(parts, slots, inv_slots.reshape(mixed))
    parts = exchange(parts.reshape(members, -1, LANES), GROUP)
    mixed = parts.reshape(mixed)
    solved_shape = (block_one[0] // members, LANES)
    parts, solved_one = kernel_call(couple_up_kernel, [(members, *piece), solved_shape], "couple_up")(
        parts, root, couple_sep1
    )
    parts = spread(jnp.sum(exchange(parts, GROUP), axis=0), LINE)
    (parts,) = kernel_call(solve_root_kernel, [block_root], "solve_root")(parts, mixed)
    solved_root = jnp.sum(exchange(parts.reshape(members, -1, LANES), GROUP), axis=0)
    solved_root = spread(solved_root, GROUP).reshape(block_root)
    (parts,) = kernel_call(lift_root_kernel, [(lax.axis_size(LINE), *piece)], "lift_root")(solved_root, mixed)
    x_root = spread(jnp.sum(exchange(parts, LINE), axis=0), GROUP)
    (rest,) = kernel_call(rest_one_kernel, [solved_one.shape], "rest_one")(x_root, solved_one, couple_sep1)
    rest = spread(rest, GROUP).reshape(block_one)
    (parts,) = kernel_call(lift_one_kernel, [(lax.axis_size(HALF), *piece)], "lift_one", [flat_one])(rest, slots)
    x_one = spread(jnp.sum(exchange(parts, HALF), axis=0), GROUP)
    return backward(x_one, x_root, solved_local, inv_local, couple_local, row_index, rows_one, rows_root, own_index)


def solution(mesh):
    leaf, blk = mesh.devices.shape
    regrouped = Mesh(mesh.devices.reshape(2, leaf // 8, 2, 2, blk), EVERY)
    spec = P(EVERY, None)
    return jax.shard_map(shards, mesh=regrouped, in_specs=(spec,) * 9, out_specs=(spec,) * 3, check_vma=False)
```

```python
import functools

import jax
import jax.numpy as jnp
from jax import lax
from jax.experimental import pallas as pl
from jax.experimental.pallas import tpu as pltpu
from jax.sharding import Mesh
from jax.sharding import PartitionSpec as P

GROUP = ("near", "core", "blk")
HALF = ("pair",)
LINE = ("half", "pair")
EVERY = LINE + GROUP

VMEM = pl.BlockSpec(memory_space=pltpu.VMEM)
SMEM = pl.BlockSpec(memory_space=pltpu.SMEM)
HBM = pl.BlockSpec(memory_space=pltpu.HBM)
LANES = 128
UNROLL = 32


def halves(value):
    high = value.astype(jnp.bfloat16)
    return high, (value - high.astype(jnp.float32)).astype(jnp.bfloat16)


def dot16(left, right):
    return jnp.dot(left, right, preferred_element_type=jnp.float32)


def tall_product(left, right):
    n = right.shape[1]
    left_high, left_low = halves(left)
    right_high, right_low = halves(right)
    both = dot16(left_high, jnp.concatenate([right_high, right_low], axis=1))
    return both[:, :n] + (both[:, n:] + dot16(left_low, right_high))


def wide_product(left, right):
    m = left.shape[0]
    left_high, left_low = halves(left)
    right_high, right_low = halves(right)
    both = dot16(jnp.concatenate([left_high, left_low], axis=0), right_high)
    return both[:m] + (both[m:] + dot16(left_high, right_low))


PILES = 4


def lane_piles(rows):
    return lax.broadcasted_iota(jnp.int32, (rows, LANES), 1) // (LANES // PILES)


def deal(stacks, width):
    granule = lax.broadcasted_iota(jnp.int32, stacks[0].shape, 1) // width
    turned = [stack if k == 0 else pltpu.roll(stack, width * k, 1) for k, stack in enumerate(stacks)]
    count = LANES // width
    for first in range(count):
        row = jnp.zeros_like(stacks[0])
        for k, stack in enumerate(turned):
            row = jnp.where(granule == (first + k) % count, stack, row)
        yield row if first == 0 else pltpu.roll(row, LANES - width * first, 1)


def fetch(pairs, sems):
    copies = [pltpu.make_async_copy(source, target, sems.at[k]) for k, (source, target) in enumerate(pairs)]
    for copy in copies:
        copy.start()
    return copies


def own_position(axes):
    position = lax.axis_index(axes[0])
    for axis in axes[1:]:
        position = position * lax.axis_size(axis) + lax.axis_index(axis)
    return position


def forward_kernel(
    position, rhs, inv, couple, index, rhs_one, inv_one, slots, solved, lifted_out,
    rhs_here, inv_here, couple_here, index_here, index_wide, rhs_one_here, inv_one_here, update, lifted, sems,
):
    quarter = couple.shape[1] // 4
    quarters = [slice(k * quarter, (k + 1) * quarter) for k in range(4)]
    copies = fetch(
        [
            (rhs, rhs_here),
            (inv_one, inv_one_here),
            (inv, inv_here),
            (index, index_here),
            (index, index_wide),
            *[(couple.at[:, columns], couple_here.at[:, columns]) for columns in quarters],
            (rhs_one, rhs_one_here),
        ],
        sems,
    )
    get_rhs, get_inv_one, get_inv, get_index, get_index_wide, *get_couple, get_rhs_one = copies
    samples = rhs.shape[0]
    rows_one = rhs_one.shape[0]
    sep_rows = inv_one.shape[1]
    pile = sep_rows // PILES
    depth = slots.shape[1] - rows_one // 2
    clear(update, 0, sep_rows)

    get_rhs.wait()
    get_inv_one.wait()
    for first in range(0, pile, LANES):
        columns = [slice(g * pile + first, g * pile + first + LANES) for g in range(PILES)]
        stacks = [inv_one_here[r : r + rows_one // 2, c] for r in (0, rows_one // 2) for c in columns]
        for k, row in enumerate(deal(stacks, depth)):
            slots[first // depth + k, depth:, :] = row

    get_inv.wait()
    y = tall_product(inv_here[...], rhs_here[...].T)
    solved[...] = y
    y = -y.T
    get_index.wait()
    get_index_wide.wait()
    low = jnp.sum((index_wide[...] < sep_rows).astype(jnp.int32))
    for copy, columns in zip(get_couple, quarters, strict=True):
        copy.wait()
        part = wide_product(y, couple_here[:, columns])
        lifted_out[:, columns] = part
        lifted[columns, :] = jnp.concatenate([part] * PILES, axis=0).T

    scatter_rows(update, lifted, index_here, 0, (low + UNROLL - 1) // UNROLL)

    get_rhs_one.wait()
    own_one = pl.ds(pl.multiple_of(position() % (sep_rows // rows_one) * rows_one, rows_one), rows_one)
    update[own_one, :] = update[own_one, :] + jnp.concatenate([rhs_one_here[...]] * PILES, axis=1)
    for member in range(slots.shape[0]):
        slots[member, :depth, :] = merged(update, 0, member, depth, pile)


def clear(target, start, rows):
    @pl.loop(0, rows // 512)
    def _(step):
        target[pl.ds(pl.multiple_of(start + step * 512, 512), 512), :] = jnp.zeros((512, LANES), jnp.float32)


def scatter_rows(target, source, index, first, last):
    @pl.loop(first, last)
    def _(step):
        base = pl.multiple_of(step * UNROLL, UNROLL)
        for k in range(UNROLL):
            target[pl.ds(index[0, base + k], 1), :] = source[pl.ds(base + k, 1), :]


def merged(update, base, member, depth, pile):
    starts = [base + g * pile + member * depth for g in range(PILES)]
    piles = lane_piles(depth)
    piece = update[starts[0] : starts[0] + depth, :]
    for g in range(1, PILES):
        piece = jnp.where(piles == g, update[starts[g] : starts[g] + depth, :], piece)
    return piece


def root_kernel(
    position, lifted_wide, index, rhs_root, inv_root, inv_slots, root,
    index_here, index_wide, rhs_root_here, inv_root_here, update, lifted, sems,
):
    copies = fetch(
        [(index, index_here), (index, index_wide), (rhs_root, rhs_root_here), (inv_root, inv_root_here)], sems
    )
    rows_root = rhs_root.shape[0]
    sep_rows = inv_root.shape[1]
    pile = sep_rows // PILES
    depth = root.shape[1]
    clear(update, sep_rows, sep_rows)
    lifted[...] = jnp.concatenate([lifted_wide[...]] * PILES, axis=0).T
    for copy in copies:
        copy.wait()
    low = jnp.sum((index_wide[...] < sep_rows).astype(jnp.int32))
    scatter_rows(update, lifted, index_here, low // UNROLL, index.shape[1] // UNROLL)
    own_root = pl.ds(pl.multiple_of(sep_rows + position() * rows_root, rows_root), rows_root)
    update[own_root, :] = update[own_root, :] + jnp.concatenate([rhs_root_here[...]] * PILES, axis=1)
    for member in range(root.shape[0]):
        root[member] = merged(update, sep_rows, member, depth, pile)
    for first in range(0, pile, LANES):
        columns = [slice(g * pile + first, g * pile + first + LANES) for g in range(PILES)]
        stacks = [inv_root_here[r : r + rows_root // 2, c] for r in (0, rows_root // 2) for c in columns]
        for k, row in enumerate(deal(stacks, depth)):
            inv_slots[first // depth + k, rows_root // 2 :, :] = row


def like(array):
    return pltpu.VMEM(array.shape, array.dtype)


def forward(rhs_local, inv_local, couple_local, row_index, rhs_sep1, inv_sep1, rhs_sep0, inv_sep0, position):
    samples = rhs_local.shape[1]
    members = lax.axis_size(GROUP)
    depth = inv_sep1.shape[1] // members // PILES
    slot_rows = depth + inv_sep1.shape[0] // 2
    given = (rhs_local.T, inv_local, couple_local, row_index, rhs_sep1, inv_sep1)
    wide = pltpu.VMEM((couple_local.shape[1], LANES), jnp.float32)
    update = pltpu.VMEM((2 * inv_sep1.shape[1], LANES), jnp.float32)
    index_here = pltpu.SMEM(row_index.shape, row_index.dtype)
    slots, solved, lifted = pl.pallas_call(
        functools.partial(forward_kernel, position),
        out_shape=(
            jax.ShapeDtypeStruct((members, slot_rows, LANES), jnp.float32),
            jax.ShapeDtypeStruct(rhs_local.shape, jnp.float32),
            jax.ShapeDtypeStruct((samples, couple_local.shape[1]), jnp.float32),
        ),
        in_specs=[HBM] * len(given),
        out_specs=(VMEM, VMEM, VMEM),
        scratch_shapes=[
            *[like(array) for array in given[:3]],
            index_here,
            like(row_index),
            like(rhs_sep1),
            like(inv_sep1),
            update,
            wide,
            pltpu.SemaphoreType.DMA((10,)),
        ],
        compiler_params=pltpu.CompilerParams(vmem_limit_bytes=63 * 2**20),
        name="local_forward",
    )(*given)
    inv_slots, root = pl.pallas_call(
        functools.partial(root_kernel, position),
        out_shape=(
            jax.ShapeDtypeStruct((members, inv_sep0.shape[0], LANES), jnp.float32),
            jax.ShapeDtypeStruct((members, depth, LANES), jnp.float32),
        ),
        in_specs=[VMEM, HBM, HBM, HBM],
        out_specs=(VMEM, VMEM),
        scratch_shapes=[
            index_here,
            like(row_index),
            like(rhs_sep0),
            like(inv_sep0),
            update,
            wide,
            pltpu.SemaphoreType.DMA((4,)),
        ],
        compiler_params=pltpu.CompilerParams(vmem_limit_bytes=24 * 2**20),
        name="local_root",
    )(lifted, row_index, rhs_sep0, inv_sep0)
    return slots, inv_slots, root, solved


def spread_rows(target, base, source):
    members, depth, _ = source.shape
    piles = lane_piles(LANES)
    step = LANES // depth
    for member in range(0, members, step):
        rows = source[member : member + step].reshape(LANES, LANES)
        for g in range(PILES):
            start = base + (g * members + member) * depth
            target[start : start + LANES, :] = jnp.where(piles == g, rows, 0.0)


def folded(wide):
    samples = LANES // PILES
    total_here = wide[:, :samples]
    for g in range(1, PILES):
        total_here = total_here + wide[:, g * samples : (g + 1) * samples]
    return total_here


def own_rows(table, start, rows):
    return folded(table[pl.ds(pl.multiple_of(start, rows), rows), :])


def gather_rows(target, source, index, first, last):
    @pl.loop(first, last)
    def _(step):
        base = pl.multiple_of(step * UNROLL, UNROLL)
        for k in range(UNROLL):
            target[pl.ds(base + k, 1), :] = source[pl.ds(index[0, base + k], 1), :]


def backward_kernel(
    position, one, root, solved, inv, couple, index, x_local, own_one, own_root,
    one_here, root_here, solved_here, inv_here, couple_here, index_here, ancestor, above, sems,
):
    get_one, get_root, get_index, get_couple, get_solved, get_inv = fetch(
        [
            (one, one_here),
            (root, root_here),
            (index, index_here),
            (couple, couple_here),
            (solved, solved_here),
            (inv, inv_here),
        ],
        sems,
    )
    sep_rows = PILES * one.shape[0] * one.shape[1]
    rows_one = own_one.shape[0]
    rows_root = own_root.shape[0]
    get_one.wait()
    spread_rows(ancestor, 0, one_here)
    get_root.wait()
    spread_rows(ancestor, sep_rows, root_here)
    here = position()
    own_one[...] = own_rows(ancestor, here % (sep_rows // rows_one) * rows_one, rows_one)
    own_root[...] = own_rows(ancestor, sep_rows + here * rows_root, rows_root)
    get_index.wait()
    gather_rows(above, ancestor, index_here, 0, index.shape[1] // UNROLL)
    get_couple.wait()
    get_solved.wait()
    rest = solved_here[...] - folded(tall_product(couple_here[...], above[...]))
    get_inv.wait()
    x_local[...] = wide_product(rest.T, inv_here[...])


def backward(one, root, solved, inv_local, couple_local, row_index, rows_one, rows_root, position):
    samples = solved.shape[1]
    x_local, own_one, own_root = pl.pallas_call(
        functools.partial(backward_kernel, position),
        out_shape=(
            jax.ShapeDtypeStruct(solved.shape[::-1], jnp.float32),
            jax.ShapeDtypeStruct((rows_one, samples), jnp.float32),
            jax.ShapeDtypeStruct((rows_root, samples), jnp.float32),
        ),
        in_specs=[HBM] * 6,
        out_specs=(VMEM, VMEM, VMEM),
        scratch_shapes=[
            like(one),
            like(root),
            like(solved),
            like(inv_local),
            like(couple_local),
            pltpu.SMEM(row_index.shape, row_index.dtype),
            pltpu.VMEM((2 * PILES * one.shape[0] * one.shape[1], LANES), jnp.float32),
            pltpu.VMEM((couple_local.shape[1], LANES), jnp.float32),
            pltpu.SemaphoreType.DMA((6,)),
        ],
        compiler_params=pltpu.CompilerParams(vmem_limit_bytes=63 * 2**20),
        name="local_backward",
    )(one, root, solved, inv_local, couple_local, row_index)
    return x_local.T, own_one, own_root


def own_index():
    return own_position(EVERY)


def kernel_call(body, out_shapes, name, scratch=()):
    return pl.pallas_call(
        body,
        out_shape=tuple(jax.ShapeDtypeStruct(shape, jnp.float32) for shape in out_shapes),
        scratch_shapes=[pltpu.VMEM(shape, jnp.float32) for shape in scratch],
        compiler_params=pltpu.CompilerParams(vmem_limit_bytes=16 * 2**20),
        name=name,
    )


def summed(parts):
    terms = [parts[k] for k in range(parts.shape[0])]
    while len(terms) > 1:
        terms = [a + b for a, b in zip(terms[::2], terms[1::2], strict=True)]
    return terms[0]


def rows_of(piece):
    samples = LANES // PILES
    return jnp.concatenate([piece[:, g * samples : (g + 1) * samples] for g in range(PILES)], axis=0)


def piece_of(rows):
    depth = rows.shape[0] // PILES
    return jnp.concatenate([rows[g * depth : (g + 1) * depth] for g in range(PILES)], axis=1)


def inv_one_block(slots):
    piece = slots[:, slots.shape[1] - 8 :, :]
    return piece.reshape(piece.shape[0] * 8, LANES)


def inv_root_block(mixed):
    members = mixed.shape[0] // 8
    return jnp.concatenate([mixed[pl.ds(4 + i, members, stride=8), :] for i in range(4)], axis=0)


def twice(rows):
    blank = jnp.zeros_like(rows)
    return jnp.concatenate(
        [jnp.concatenate([rows, blank], axis=1), jnp.concatenate([blank, rows], axis=1)],
        axis=0,
    )


def solve_one_kernel(parts, slots, inv_slots, out, scratch):
    scratch[...] = tall_product(inv_one_block(slots), twice(rows_of(summed(parts))))
    members = scratch.shape[0] // 8
    out[...] = inv_slots[...]
    for i in range(4):
        pieces = [scratch[pl.ds(4 * h + i, members, stride=8), :] for h in range(2)]
        out[pl.ds(i, members, stride=8), :] = jnp.concatenate(pieces, axis=1)


def couple_up_kernel(parts, root, couple, out, solved):
    samples = LANES // PILES
    total_here = summed(parts)[: solved.shape[0]]
    solved[...] = total_here
    flipped = total_here.T
    order = [(g, h) for g in range(2) for h in range(2)]
    y = jnp.concatenate([flipped[(2 * h + g) * samples : (2 * h + g + 1) * samples] for g, h in order], axis=1)
    lifted = wide_product(y, couple[...])
    pile = lifted.shape[1] // PILES
    lifted = jnp.concatenate([lifted[:, g * pile : (g + 1) * pile] for g in range(PILES)], axis=0).T
    out[...] = root[...] - lifted.reshape(root.shape)


def solve_root_kernel(parts, mixed, out):
    y = tall_product(inv_root_block(mixed), twice(rows_of(summed(parts))))
    rows = out.shape[0]
    out[...] = jnp.concatenate([y[:rows], y[rows:]], axis=1)


def lift_root_kernel(solved, mixed, out):
    half = LANES // 2
    samples = LANES // PILES
    flipped = solved[...].T
    y = jnp.concatenate([flipped[:half], flipped[half:]], axis=1)
    every = wide_product(y, inv_root_block(mixed))
    piece = piece_of((every[:samples, :half] + every[samples:, half:]).T)
    for member in range(out.shape[0]):
        out[member] = piece


def rest_one_kernel(root, solved, couple, out):
    samples = LANES // PILES
    rows, columns = couple.shape
    pile = columns // PILES
    stacked = jnp.concatenate([couple[:, g * pile : (g + 1) * pile] for g in range(PILES)], axis=0)
    every = wide_product(stacked, root[...].reshape(pile, LANES))
    down = every[:rows, :samples]
    for g in range(1, PILES):
        down = down + every[g * rows : (g + 1) * rows, g * samples : (g + 1) * samples]
    order = [(h, g) for h in range(2) for g in range(2)]
    out[...] = solved[...] - jnp.concatenate([down[8 * g + 4 * h : 8 * g + 4 * h + 4] for h, g in order], axis=1)


def lift_one_kernel(rest, slots, out, scratch):
    samples = LANES // PILES
    members = rest.shape[0] // 4
    for i in range(4):
        pieces = rest[pl.ds(i, members, stride=4), :]
        for h in range(2):
            scratch[pl.ds(4 * h + i, members, stride=8), :] = pieces[:, 2 * samples * h : 2 * samples * (h + 1)]
    every = wide_product(scratch[...].T, inv_one_block(slots))
    half = LANES // 2
    piece = piece_of((every[:samples, :half] + every[samples:, half:]).T)
    for member in range(out.shape[0]):
        out[member] = piece


def exchange(slots, axes):
    return lax.all_to_all(slots, axes, 0, 0)


def spread(value, axes):
    return exchange(jnp.broadcast_to(value[None], (lax.axis_size(axes),) + value.shape), axes)


def shards(
    rhs_local,
    inv_local,
    couple_local,
    row_index,
    rhs_sep1,
    inv_sep1,
    couple_sep1,
    rhs_sep0,
    inv_sep0,
):
    samples = rhs_local.shape[1]
    members = lax.axis_size(GROUP)
    rows_one, rows_root = rhs_sep1.shape[0], rhs_sep0.shape[0]
    piece = (inv_sep0.shape[1] // members // PILES, LANES)
    block_one = (members * rows_one * samples // LANES, LANES)
    block_root = (members * rows_root * samples // LANES, LANES)
    flat_one = (members * rows_one // 2, 2 * samples)

    slots, inv_slots, root, solved_local = forward(
        rhs_local, inv_local, couple_local, row_index, rhs_sep1, inv_sep1, rhs_sep0, inv_sep0, own_index
    )
    slots, inv_slots, root = lax.optimization_barrier((exchange(slots, GROUP), inv_slots, root))
    parts = spread(jnp.sum(slots[:, : piece[0]], axis=0), HALF)
    mixed = (members * inv_slots.shape[1], LANES)
    (parts,) = kernel_call(solve_one_kernel, [mixed], "solve_one", [flat_one])(parts, slots, inv_slots.reshape(mixed))
    parts = exchange(parts.reshape(members, -1, LANES), GROUP)
    mixed = parts.reshape(mixed)
    solved_shape = (block_one[0] // members, LANES)
    parts, solved_one = kernel_call(couple_up_kernel, [(members, *piece), solved_shape], "couple_up")(
        parts, root, couple_sep1
    )
    parts = spread(jnp.sum(exchange(parts, GROUP), axis=0), LINE)
    (parts,) = kernel_call(solve_root_kernel, [block_root], "solve_root")(parts, mixed)
    solved_root = jnp.sum(exchange(parts.reshape(members, -1, LANES), GROUP), axis=0)
    solved_root = spread(solved_root, GROUP).reshape(block_root)
    (parts,) = kernel_call(lift_root_kernel, [(lax.axis_size(LINE), *piece)], "lift_root")(solved_root, mixed)
    x_root = spread(jnp.sum(exchange(parts, LINE), axis=0), GROUP)
    (rest,) = kernel_call(rest_one_kernel, [solved_one.shape], "rest_one")(x_root, solved_one, couple_sep1)
    rest = spread(rest, GROUP).reshape(block_one)
    (parts,) = kernel_call(lift_one_kernel, [(lax.axis_size(HALF), *piece)], "lift_one", [flat_one])(rest, slots)
    x_one = spread(jnp.sum(exchange(parts, HALF), axis=0), GROUP)
    return backward(x_one, x_root, solved_local, inv_local, couple_local, row_index, rows_one, rows_root, own_index)


def solution(mesh):
    leaf, blk = mesh.devices.shape
    regrouped = Mesh(mesh.devices.reshape(2, leaf // 8, 2, 2, blk), EVERY)
    spec = P(EVERY, None)
    return jax.shard_map(shards, mesh=regrouped, in_specs=(spec,) * 9, out_specs=(spec,) * 3, check_vma=False)
```

```python
import functools

import jax
import jax.numpy as jnp
from jax import lax
from jax.experimental import pallas as pl
from jax.experimental.pallas import tpu as pltpu
from jax.sharding import Mesh
from jax.sharding import PartitionSpec as P

GROUP = ("near", "core", "blk")
HALF = ("pair",)
LINE = ("half", "pair")
EVERY = LINE + GROUP

VMEM = pl.BlockSpec(memory_space=pltpu.VMEM)
SMEM = pl.BlockSpec(memory_space=pltpu.SMEM)
HBM = pl.BlockSpec(memory_space=pltpu.HBM)
LANES = 128
UNROLL = 32


def halves(value):
    high = value.astype(jnp.bfloat16)
    return high, (value - high.astype(jnp.float32)).astype(jnp.bfloat16)


def dot16(left, right):
    return jnp.dot(left, right, preferred_element_type=jnp.float32)


def tall_product(left, right):
    n = right.shape[1]
    left_high, left_low = halves(left)
    right_high, right_low = halves(right)
    both = dot16(left_high, jnp.concatenate([right_high, right_low], axis=1))
    return both[:, :n] + (both[:, n:] + dot16(left_low, right_high))


def wide_product(left, right):
    m = left.shape[0]
    left_high, left_low = halves(left)
    right_high, right_low = halves(right)
    both = dot16(jnp.concatenate([left_high, left_low], axis=0), right_high)
    return both[:m] + (both[m:] + dot16(left_high, right_low))


PILES = 4


def lane_piles(rows):
    return lax.broadcasted_iota(jnp.int32, (rows, LANES), 1) // (LANES // PILES)


def deal(stacks, width):
    granule = lax.broadcasted_iota(jnp.int32, stacks[0].shape, 1) // width
    turned = [stack if k == 0 else pltpu.roll(stack, width * k, 1) for k, stack in enumerate(stacks)]
    count = LANES // width
    for first in range(count):
        row = jnp.zeros_like(stacks[0])
        for k, stack in enumerate(turned):
            row = jnp.where(granule == (first + k) % count, stack, row)
        yield row if first == 0 else pltpu.roll(row, LANES - width * first, 1)


def fetch(pairs, sems):
    copies = [pltpu.make_async_copy(source, target, sems.at[k]) for k, (source, target) in enumerate(pairs)]
    for copy in copies:
        copy.start()
    return copies


def own_position(axes):
    position = lax.axis_index(axes[0])
    for axis in axes[1:]:
        position = position * lax.axis_size(axis) + lax.axis_index(axis)
    return position


def forward_kernel(
    position, rhs, inv, couple, index, rhs_one, inv_one, slots, solved, lifted_out,
    rhs_here, inv_here, couple_here, index_here, index_wide, rhs_one_here, inv_one_here, update, lifted,
    slots_here, solved_here, lifted_here, sems, out_sems,
):
    quarter = couple.shape[1] // 4
    quarters = [slice(k * quarter, (k + 1) * quarter) for k in range(4)]
    copies = fetch(
        [
            (index, index_here),
            (index, index_wide),
            (inv_one, inv_one_here),
            (rhs, rhs_here),
            (inv, inv_here),
            *[(couple.at[:, columns], couple_here.at[:, columns]) for columns in quarters],
            (rhs_one, rhs_one_here),
        ],
        sems,
    )
    get_index, get_index_wide, get_inv_one, get_rhs, get_inv, *get_couple, get_rhs_one = copies
    samples = rhs.shape[0]
    rows_one = rhs_one.shape[0]
    sep_rows = inv_one.shape[1]
    pile = sep_rows // PILES
    depth = slots.shape[1] - rows_one // 2
    clear(update, 0, sep_rows)

    get_index.wait()
    get_index_wide.wait()
    low = jnp.sum((index_wide[...] < sep_rows).astype(jnp.int32))
    get_inv_one.wait()
    for first in range(0, pile, LANES):
        columns = [slice(g * pile + first, g * pile + first + LANES) for g in range(PILES)]
        stacks = [inv_one_here[r : r + rows_one // 2, c] for r in (0, rows_one // 2) for c in columns]
        for k, row in enumerate(deal(stacks, depth)):
            slots_here[first // depth + k, depth:, :] = row
    puts = fetch([(slots_here.at[:, depth:, :], slots.at[:, depth:, :])], out_sems.at[:1])

    get_rhs.wait()
    get_inv.wait()
    y = tall_product(inv_here[...], rhs_here[...].T).T
    solved_here[...] = y
    puts += fetch([(solved_here, solved)], out_sems.at[1:2])
    y = -y
    for copy, columns in zip(get_couple, quarters, strict=True):
        copy.wait()
        part = wide_product(y, couple_here[:, columns])
        lifted_here[:, columns] = part
        lifted[columns, :] = jnp.concatenate([part] * PILES, axis=0).T

    puts += fetch([(lifted_here, lifted_out)], out_sems.at[2:3])

    scatter_rows(update, lifted, index_here, 0, (low + UNROLL - 1) // UNROLL)

    get_rhs_one.wait()
    own_one = pl.ds(pl.multiple_of(position() % (sep_rows // rows_one) * rows_one, rows_one), rows_one)
    update[own_one, :] = update[own_one, :] + jnp.concatenate([rhs_one_here[...]] * PILES, axis=1)
    members = slots.shape[0]
    for k in range(2):
        some = slice(k * members // 2, (k + 1) * members // 2)
        for member in range(some.start, some.stop):
            slots_here[member, :depth, :] = merged(update, 0, member, depth, pile)
        puts += fetch([(slots_here.at[some, :depth, :], slots.at[some, :depth, :])], out_sems.at[3 + k : 4 + k])
    for put in puts:
        put.wait()


def clear(target, start, rows):
    @pl.loop(0, rows // 512)
    def _(step):
        target[pl.ds(pl.multiple_of(start + step * 512, 512), 512), :] = jnp.zeros((512, LANES), jnp.float32)


def scatter_rows(target, source, index, first, last):
    @pl.loop(first, last)
    def _(step):
        base = pl.multiple_of(step * UNROLL, UNROLL)
        for k in range(UNROLL):
            target[pl.ds(index[0, base + k], 1), :] = source[pl.ds(base + k, 1), :]


def merged(update, base, member, depth, pile):
    starts = [base + g * pile + member * depth for g in range(PILES)]
    piles = lane_piles(depth)
    piece = update[starts[0] : starts[0] + depth, :]
    for g in range(1, PILES):
        piece = jnp.where(piles == g, update[starts[g] : starts[g] + depth, :], piece)
    return piece


def root_kernel(
    position, lifted_wide, index, rhs_root, inv_root, inv_slots, root,
    index_here, index_wide, rhs_root_here, inv_root_here, update, lifted, sems,
):
    copies = fetch(
        [(index, index_here), (index, index_wide), (rhs_root, rhs_root_here), (inv_root, inv_root_here)], sems
    )
    rows_root = rhs_root.shape[0]
    sep_rows = inv_root.shape[1]
    pile = sep_rows // PILES
    depth = root.shape[1]
    clear(update, sep_rows, sep_rows)
    lifted[...] = jnp.concatenate([lifted_wide[...]] * PILES, axis=0).T
    for copy in copies:
        copy.wait()
    low = jnp.sum((index_wide[...] < sep_rows).astype(jnp.int32))
    scatter_rows(update, lifted, index_here, low // UNROLL, index.shape[1] // UNROLL)
    own_root = pl.ds(pl.multiple_of(sep_rows + position() * rows_root, rows_root), rows_root)
    update[own_root, :] = update[own_root, :] + jnp.concatenate([rhs_root_here[...]] * PILES, axis=1)
    for member in range(root.shape[0]):
        root[member] = merged(update, sep_rows, member, depth, pile)
    for first in range(0, pile, LANES):
        columns = [slice(g * pile + first, g * pile + first + LANES) for g in range(PILES)]
        stacks = [inv_root_here[r : r + rows_root // 2, c] for r in (0, rows_root // 2) for c in columns]
        for k, row in enumerate(deal(stacks, depth)):
            inv_slots[first // depth + k, rows_root // 2 :, :] = row


def like(array):
    return pltpu.VMEM(array.shape, array.dtype)


def forward(rhs_local, inv_local, couple_local, row_index, rhs_sep1, inv_sep1, rhs_sep0, inv_sep0, position):
    samples = rhs_local.shape[1]
    members = lax.axis_size(GROUP)
    depth = inv_sep1.shape[1] // members // PILES
    slot_rows = depth + inv_sep1.shape[0] // 2
    given = (rhs_local.T, inv_local, couple_local, row_index, rhs_sep1, inv_sep1)
    wide = pltpu.VMEM((couple_local.shape[1], LANES), jnp.float32)
    update = pltpu.VMEM((2 * inv_sep1.shape[1], LANES), jnp.float32)
    index_here = pltpu.SMEM(row_index.shape, row_index.dtype)
    slots, solved, lifted = pl.pallas_call(
        functools.partial(forward_kernel, position),
        out_shape=(
            jax.ShapeDtypeStruct((members, slot_rows, LANES), jnp.float32),
            jax.ShapeDtypeStruct(rhs_local.shape[::-1], jnp.float32),
            jax.ShapeDtypeStruct((samples, couple_local.shape[1]), jnp.float32),
        ),
        in_specs=[HBM] * len(given),
        out_specs=(HBM, HBM, HBM),
        scratch_shapes=[
            *[like(array) for array in given[:3]],
            index_here,
            like(row_index),
            like(rhs_sep1),
            like(inv_sep1),
            update,
            wide,
            pltpu.VMEM((members, slot_rows, LANES), jnp.float32),
            pltpu.VMEM(rhs_local.shape[::-1], jnp.float32),
            pltpu.VMEM((samples, couple_local.shape[1]), jnp.float32),
            pltpu.SemaphoreType.DMA((10,)),
            pltpu.SemaphoreType.DMA((5,)),
        ],
        compiler_params=pltpu.CompilerParams(vmem_limit_bytes=63 * 2**20),
        name="local_forward",
    )(*given)
    inv_slots, root = pl.pallas_call(
        functools.partial(root_kernel, position),
        out_shape=(
            jax.ShapeDtypeStruct((members, inv_sep0.shape[0], LANES), jnp.float32),
            jax.ShapeDtypeStruct((members, depth, LANES), jnp.float32),
        ),
        in_specs=[VMEM, HBM, HBM, HBM],
        out_specs=(VMEM, VMEM),
        scratch_shapes=[
            index_here,
            like(row_index),
            like(rhs_sep0),
            like(inv_sep0),
            update,
            wide,
            pltpu.SemaphoreType.DMA((4,)),
        ],
        compiler_params=pltpu.CompilerParams(vmem_limit_bytes=24 * 2**20),
        name="local_root",
    )(lifted, row_index, rhs_sep0, inv_sep0)
    return slots, inv_slots, root, solved


def spread_rows(target, base, source):
    members, depth, _ = source.shape
    piles = lane_piles(LANES)
    step = LANES // depth
    for member in range(0, members, step):
        rows = source[member : member + step].reshape(LANES, LANES)
        for g in range(PILES):
            start = base + (g * members + member) * depth
            target[start : start + LANES, :] = jnp.where(piles == g, rows, 0.0)


def folded(wide):
    samples = LANES // PILES
    total_here = wide[:, :samples]
    for g in range(1, PILES):
        total_here = total_here + wide[:, g * samples : (g + 1) * samples]
    return total_here


def own_rows(table, start, rows):
    return folded(table[pl.ds(pl.multiple_of(start, rows), rows), :])


def gather_rows(target, source, index, first, last):
    @pl.loop(first, last)
    def _(step):
        base = pl.multiple_of(step * UNROLL, UNROLL)
        for k in range(UNROLL):
            target[pl.ds(base + k, 1), :] = source[pl.ds(index[0, base + k], 1), :]


def backward_kernel(
    position, one, root, solved, inv, couple, index, x_local, own_one, own_root,
    one_here, root_here, solved_here, inv_here, couple_here, index_here, ancestor, above, sems,
):
    get_one, get_root, get_index, get_couple, get_solved, get_inv = fetch(
        [
            (one, one_here),
            (root, root_here),
            (index, index_here),
            (couple, couple_here),
            (solved, solved_here),
            (inv, inv_here),
        ],
        sems,
    )
    sep_rows = PILES * one.shape[0] * one.shape[1]
    rows_one = own_one.shape[0]
    rows_root = own_root.shape[0]
    get_one.wait()
    spread_rows(ancestor, 0, one_here)
    get_root.wait()
    spread_rows(ancestor, sep_rows, root_here)
    here = position()
    own_one[...] = own_rows(ancestor, here % (sep_rows // rows_one) * rows_one, rows_one)
    own_root[...] = own_rows(ancestor, sep_rows + here * rows_root, rows_root)
    get_index.wait()
    gather_rows(above, ancestor, index_here, 0, index.shape[1] // UNROLL)
    get_couple.wait()
    get_solved.wait()
    rest = solved_here[...] - folded(tall_product(couple_here[...], above[...])).T
    get_inv.wait()
    x_local[...] = wide_product(rest, inv_here[...])


def backward(one, root, solved, inv_local, couple_local, row_index, rows_one, rows_root, position):
    samples = solved.shape[0]
    x_local, own_one, own_root = pl.pallas_call(
        functools.partial(backward_kernel, position),
        out_shape=(
            jax.ShapeDtypeStruct(solved.shape, jnp.float32),
            jax.ShapeDtypeStruct((rows_one, samples), jnp.float32),
            jax.ShapeDtypeStruct((rows_root, samples), jnp.float32),
        ),
        in_specs=[HBM] * 6,
        out_specs=(VMEM, VMEM, VMEM),
        scratch_shapes=[
            like(one),
            like(root),
            like(solved),
            like(inv_local),
            like(couple_local),
            pltpu.SMEM(row_index.shape, row_index.dtype),
            pltpu.VMEM((2 * PILES * one.shape[0] * one.shape[1], LANES), jnp.float32),
            pltpu.VMEM((couple_local.shape[1], LANES), jnp.float32),
            pltpu.SemaphoreType.DMA((6,)),
        ],
        compiler_params=pltpu.CompilerParams(vmem_limit_bytes=63 * 2**20),
        name="local_backward",
    )(one, root, solved, inv_local, couple_local, row_index)
    return x_local.T, own_one, own_root


def own_index():
    return own_position(EVERY)


def kernel_call(body, out_shapes, name, scratch=()):
    return pl.pallas_call(
        body,
        out_shape=tuple(jax.ShapeDtypeStruct(shape, jnp.float32) for shape in out_shapes),
        scratch_shapes=[pltpu.VMEM(shape, jnp.float32) for shape in scratch],
        compiler_params=pltpu.CompilerParams(vmem_limit_bytes=16 * 2**20),
        name=name,
    )


def summed(parts):
    terms = [parts[k] for k in range(parts.shape[0])]
    while len(terms) > 1:
        terms = [a + b for a, b in zip(terms[::2], terms[1::2], strict=True)]
    return terms[0]


def rows_of(piece):
    samples = LANES // PILES
    return jnp.concatenate([piece[:, g * samples : (g + 1) * samples] for g in range(PILES)], axis=0)


def piece_of(rows):
    depth = rows.shape[0] // PILES
    return jnp.concatenate([rows[g * depth : (g + 1) * depth] for g in range(PILES)], axis=1)


def inv_one_block(slots):
    piece = slots[:, slots.shape[1] - 8 :, :]
    return piece.reshape(piece.shape[0] * 8, LANES)


def inv_root_block(mixed):
    members = mixed.shape[0] // 8
    return jnp.concatenate([mixed[pl.ds(4 + i, members, stride=8), :] for i in range(4)], axis=0)


def twice(rows):
    blank = jnp.zeros_like(rows)
    return jnp.concatenate(
        [jnp.concatenate([rows, blank], axis=1), jnp.concatenate([blank, rows], axis=1)],
        axis=0,
    )


def solve_one_kernel(parts, slots, inv_slots, out, scratch):
    scratch[...] = tall_product(inv_one_block(slots), twice(rows_of(summed(parts))))
    members = scratch.shape[0] // 8
    out[...] = inv_slots[...]
    for i in range(4):
        pieces = [scratch[pl.ds(4 * h + i, members, stride=8), :] for h in range(2)]
        out[pl.ds(i, members, stride=8), :] = jnp.concatenate(pieces, axis=1)


def couple_up_kernel(parts, root, couple, out, solved):
    samples = LANES // PILES
    total_here = summed(parts)[: solved.shape[0]]
    solved[...] = total_here
    flipped = total_here.T
    order = [(g, h) for g in range(2) for h in range(2)]
    y = jnp.concatenate([flipped[(2 * h + g) * samples : (2 * h + g + 1) * samples] for g, h in order], axis=1)
    pile = couple.shape[1] // PILES
    members = LANES // root.shape[1]
    for first in range(0, pile, LANES):
        columns = [slice(g * pile + first, g * pile + first + LANES) for g in range(PILES)]
        lifted = wide_product(y, jnp.concatenate([couple[:, c] for c in columns], axis=1))
        lifted = jnp.concatenate([lifted[:, g * LANES : (g + 1) * LANES] for g in range(PILES)], axis=0).T
        some = slice(first // LANES * members, (first // LANES + 1) * members)
        out[some] = root[some] - lifted.reshape(members, *root.shape[1:])


def solve_root_kernel(parts, mixed, out):
    y = tall_product(inv_root_block(mixed), twice(rows_of(summed(parts))))
    rows = out.shape[0]
    out[...] = jnp.concatenate([y[:rows], y[rows:]], axis=1)


def lift_root_kernel(solved, mixed, out):
    half = LANES // 2
    samples = LANES // PILES
    flipped = solved[...].T
    y = jnp.concatenate([flipped[:half], flipped[half:]], axis=1)
    every = wide_product(y, inv_root_block(mixed))
    piece = piece_of((every[:samples, :half] + every[samples:, half:]).T)
    for member in range(out.shape[0]):
        out[member] = piece


def rest_one_kernel(root, solved, couple, out):
    samples = LANES // PILES
    rows, columns = couple.shape
    pile = columns // PILES
    stacked = jnp.concatenate([couple[:, g * pile : (g + 1) * pile] for g in range(PILES)], axis=0)
    every = wide_product(stacked, root[...].reshape(pile, LANES))
    down = every[:rows, :samples]
    for g in range(1, PILES):
        down = down + every[g * rows : (g + 1) * rows, g * samples : (g + 1) * samples]
    order = [(h, g) for h in range(2) for g in range(2)]
    out[...] = solved[...] - jnp.concatenate([down[8 * g + 4 * h : 8 * g + 4 * h + 4] for h, g in order], axis=1)


def lift_one_kernel(rest, slots, out, scratch):
    samples = LANES // PILES
    members = rest.shape[0] // 4
    for i in range(4):
        pieces = rest[pl.ds(i, members, stride=4), :]
        for h in range(2):
            scratch[pl.ds(4 * h + i, members, stride=8), :] = pieces[:, 2 * samples * h : 2 * samples * (h + 1)]
    every = wide_product(scratch[...].T, inv_one_block(slots))
    half = LANES // 2
    piece = piece_of((every[:samples, :half] + every[samples:, half:]).T)
    for member in range(out.shape[0]):
        out[member] = piece


def exchange(slots, axes):
    return lax.all_to_all(slots, axes, 0, 0)


def spread(value, axes):
    return exchange(jnp.broadcast_to(value[None], (lax.axis_size(axes),) + value.shape), axes)


def shards(
    rhs_local,
    inv_local,
    couple_local,
    row_index,
    rhs_sep1,
    inv_sep1,
    couple_sep1,
    rhs_sep0,
    inv_sep0,
):
    samples = rhs_local.shape[1]
    members = lax.axis_size(GROUP)
    rows_one, rows_root = rhs_sep1.shape[0], rhs_sep0.shape[0]
    piece = (inv_sep0.shape[1] // members // PILES, LANES)
    block_one = (members * rows_one * samples // LANES, LANES)
    block_root = (members * rows_root * samples // LANES, LANES)
    flat_one = (members * rows_one // 2, 2 * samples)

    slots, inv_slots, root, solved_local = forward(
        rhs_local, inv_local, couple_local, row_index, rhs_sep1, inv_sep1, rhs_sep0, inv_sep0, own_index
    )
    slots, inv_slots, root = lax.optimization_barrier((exchange(slots, GROUP), inv_slots, root))
    parts = spread(jnp.sum(slots[:, : piece[0]], axis=0), HALF)
    mixed = (members * inv_slots.shape[1], LANES)
    (parts,) = kernel_call(solve_one_kernel, [mixed], "solve_one", [flat_one])(parts, slots, inv_slots.reshape(mixed))
    parts = exchange(parts.reshape(members, -1, LANES), GROUP)
    mixed = parts.reshape(mixed)
    solved_shape = (block_one[0] // members, LANES)
    parts, solved_one = kernel_call(couple_up_kernel, [(members, *piece), solved_shape], "couple_up")(
        parts, root, couple_sep1
    )
    parts = spread(jnp.sum(exchange(parts, GROUP), axis=0), LINE)
    (parts,) = kernel_call(solve_root_kernel, [block_root], "solve_root")(parts, mixed)
    solved_root = jnp.sum(exchange(parts.reshape(members, -1, LANES), GROUP), axis=0)
    solved_root = spread(solved_root, GROUP).reshape(block_root)
    (parts,) = kernel_call(lift_root_kernel, [(lax.axis_size(LINE), *piece)], "lift_root")(solved_root, mixed)
    x_root = spread(jnp.sum(exchange(parts, LINE), axis=0), GROUP)
    (rest,) = kernel_call(rest_one_kernel, [solved_one.shape], "rest_one")(x_root, solved_one, couple_sep1)
    rest = spread(rest, GROUP).reshape(block_one)
    (parts,) = kernel_call(lift_one_kernel, [(lax.axis_size(HALF), *piece)], "lift_one", [flat_one])(rest, slots)
    x_one = spread(jnp.sum(exchange(parts, HALF), axis=0), GROUP)
    return backward(x_one, x_root, solved_local, inv_local, couple_local, row_index, rows_one, rows_root, own_index)


def solution(mesh):
    leaf, blk = mesh.devices.shape
    regrouped = Mesh(mesh.devices.reshape(2, leaf // 8, 2, 2, blk), EVERY)
    spec = P(EVERY, None)
    return jax.shard_map(shards, mesh=regrouped, in_specs=(spec,) * 9, out_specs=(spec,) * 3, check_vma=False)
```

```python
import functools

import jax
import jax.numpy as jnp
from jax import lax
from jax.experimental import pallas as pl
from jax.experimental.pallas import tpu as pltpu
from jax.sharding import Mesh
from jax.sharding import PartitionSpec as P

GROUP = ("near", "core", "blk")
HALF = ("pair",)
LINE = ("half", "pair")
EVERY = LINE + GROUP

VMEM = pl.BlockSpec(memory_space=pltpu.VMEM)
SMEM = pl.BlockSpec(memory_space=pltpu.SMEM)
HBM = pl.BlockSpec(memory_space=pltpu.HBM)
LANES = 128
UNROLL = 32
WIDE = 128


def halves(value):
    high = value.astype(jnp.bfloat16)
    return high, (value - high.astype(jnp.float32)).astype(jnp.bfloat16)


def dot16(left, right):
    return jnp.dot(left, right, preferred_element_type=jnp.float32)


def tall_product(left, right):
    n = right.shape[1]
    left_high, left_low = halves(left)
    right_high, right_low = halves(right)
    both = dot16(left_high, jnp.concatenate([right_high, right_low], axis=1))
    return both[:, :n] + (both[:, n:] + dot16(left_low, right_high))


def wide_product(left, right):
    m = left.shape[0]
    left_high, left_low = halves(left)
    right_high, right_low = halves(right)
    both = dot16(jnp.concatenate([left_high, left_low], axis=0), right_high)
    return both[:m] + (both[m:] + dot16(left_high, right_low))


PILES = 4


def lane_piles(rows):
    return lax.broadcasted_iota(jnp.int32, (rows, LANES), 1) // (LANES // PILES)


def deal(stacks, width):
    granule = lax.broadcasted_iota(jnp.int32, stacks[0].shape, 1) // width
    turned = [stack if k == 0 else pltpu.roll(stack, width * k, 1) for k, stack in enumerate(stacks)]
    count = LANES // width
    for first in range(count):
        row = jnp.zeros_like(stacks[0])
        for k, stack in enumerate(turned):
            row = jnp.where(granule == (first + k) % count, stack, row)
        yield row if first == 0 else pltpu.roll(row, LANES - width * first, 1)


def fetch(pairs, sems):
    copies = [pltpu.make_async_copy(source, target, sems.at[k]) for k, (source, target) in enumerate(pairs)]
    for copy in copies:
        copy.start()
    return copies


def own_position(axes):
    position = lax.axis_index(axes[0])
    for axis in axes[1:]:
        position = position * lax.axis_size(axis) + lax.axis_index(axis)
    return position


def forward_kernel(
    position, rhs, inv, couple, index, rhs_one, inv_one, slots, solved, lifted_out,
    rhs_here, inv_here, couple_here, index_here, index_wide, rhs_one_here, inv_one_here, update, lifted,
    slots_here, solved_here, lifted_here, sems, out_sems,
):
    quarter = couple.shape[1] // 4
    quarters = [slice(k * quarter, (k + 1) * quarter) for k in range(4)]
    copies = fetch(
        [
            (index, index_here),
            (index, index_wide),
            (inv_one, inv_one_here),
            (rhs, rhs_here),
            (inv, inv_here),
            *[(couple.at[:, columns], couple_here.at[:, columns]) for columns in quarters],
            (rhs_one, rhs_one_here),
        ],
        sems,
    )
    get_index, get_index_wide, get_inv_one, get_rhs, get_inv, *get_couple, get_rhs_one = copies
    samples = rhs.shape[0]
    rows_one = rhs_one.shape[0]
    sep_rows = inv_one.shape[1]
    pile = sep_rows // PILES
    depth = slots.shape[1] - rows_one // 2
    clear(update, 0, sep_rows)

    get_index.wait()
    get_index_wide.wait()
    low = jnp.sum((index_wide[...] < sep_rows).astype(jnp.int32))
    get_inv_one.wait()
    for first in range(0, pile, LANES):
        columns = [slice(g * pile + first, g * pile + first + LANES) for g in range(PILES)]
        stacks = [inv_one_here[r : r + rows_one // 2, c] for r in (0, rows_one // 2) for c in columns]
        for k, row in enumerate(deal(stacks, depth)):
            slots_here[first // depth + k, depth:, :] = row
    puts = fetch([(slots_here.at[:, depth:, :], slots.at[:, depth:, :])], out_sems.at[:1])

    get_rhs.wait()
    get_inv.wait()
    y = tall_product(inv_here[...], rhs_here[...].T).T
    solved_here[...] = y
    puts += fetch([(solved_here, solved)], out_sems.at[1:2])
    y = -y
    for copy, columns in zip(get_couple, quarters, strict=True):
        copy.wait()
        part = wide_product(y, couple_here[:, columns])
        lifted_here[:, columns] = part
        lifted[columns, :] = jnp.concatenate([part] * PILES, axis=0).T

    puts += fetch([(lifted_here, lifted_out)], out_sems.at[2:3])

    scatter_rows(update, lifted, index_here, 0, (low + UNROLL - 1) // UNROLL)

    get_rhs_one.wait()
    own_one = pl.ds(pl.multiple_of(position() % (sep_rows // rows_one) * rows_one, rows_one), rows_one)
    update[own_one, :] = update[own_one, :] + jnp.concatenate([rhs_one_here[...]] * PILES, axis=1)
    members = slots.shape[0]
    for k in range(2):
        some = slice(k * members // 2, (k + 1) * members // 2)
        for member in range(some.start, some.stop):
            slots_here[member, :depth, :] = merged(update, 0, member, depth, pile)
        puts += fetch([(slots_here.at[some, :depth, :], slots.at[some, :depth, :])], out_sems.at[3 + k : 4 + k])
    for put in puts:
        put.wait()


def clear(target, start, rows):
    @pl.loop(0, rows // 512)
    def _(step):
        target[pl.ds(pl.multiple_of(start + step * 512, 512), 512), :] = jnp.zeros((512, LANES), jnp.float32)


def scatter_rows(target, source, index, first, last):
    @pl.loop(first, last)
    def _(step):
        base = pl.multiple_of(step * UNROLL, UNROLL)
        for k in range(UNROLL):
            target[pl.ds(index[0, base + k], 1), :] = source[pl.ds(base + k, 1), :]


def merged(update, base, member, depth, pile):
    starts = [base + g * pile + member * depth for g in range(PILES)]
    piles = lane_piles(depth)
    piece = update[starts[0] : starts[0] + depth, :]
    for g in range(1, PILES):
        piece = jnp.where(piles == g, update[starts[g] : starts[g] + depth, :], piece)
    return piece


def root_kernel(
    position, lifted_wide, index, rhs_root, inv_root, inv_slots, root,
    index_here, index_wide, rhs_root_here, inv_root_here, update, lifted, sems,
):
    copies = fetch(
        [(index, index_here), (index, index_wide), (rhs_root, rhs_root_here), (inv_root, inv_root_here)], sems
    )
    rows_root = rhs_root.shape[0]
    sep_rows = inv_root.shape[1]
    pile = sep_rows // PILES
    depth = root.shape[1]
    clear(update, sep_rows, sep_rows)
    lifted[...] = jnp.concatenate([lifted_wide[...]] * PILES, axis=0).T
    for copy in copies:
        copy.wait()
    low = jnp.sum((index_wide[...] < sep_rows).astype(jnp.int32))
    scatter_rows(update, lifted, index_here, low // UNROLL, index.shape[1] // UNROLL)
    own_root = pl.ds(pl.multiple_of(sep_rows + position() * rows_root, rows_root), rows_root)
    update[own_root, :] = update[own_root, :] + jnp.concatenate([rhs_root_here[...]] * PILES, axis=1)
    for member in range(root.shape[0]):
        root[member] = merged(update, sep_rows, member, depth, pile)
    for first in range(0, pile, LANES):
        columns = [slice(g * pile + first, g * pile + first + LANES) for g in range(PILES)]
        stacks = [inv_root_here[r : r + rows_root // 2, c] for r in (0, rows_root // 2) for c in columns]
        for k, row in enumerate(deal(stacks, depth)):
            inv_slots[first // depth + k, rows_root // 2 :, :] = row


def like(array):
    return pltpu.VMEM(array.shape, array.dtype)


def forward(rhs_local, inv_local, couple_local, row_index, rhs_sep1, inv_sep1, rhs_sep0, inv_sep0, position):
    samples = rhs_local.shape[1]
    members = lax.axis_size(GROUP)
    depth = inv_sep1.shape[1] // members // PILES
    slot_rows = depth + inv_sep1.shape[0] // 2
    given = (rhs_local.T, inv_local, couple_local, row_index, rhs_sep1, inv_sep1)
    wide = pltpu.VMEM((couple_local.shape[1], LANES), jnp.float32)
    update = pltpu.VMEM((2 * inv_sep1.shape[1], LANES), jnp.float32)
    index_here = pltpu.SMEM(row_index.shape, row_index.dtype)
    slots, solved, lifted = pl.pallas_call(
        functools.partial(forward_kernel, position),
        out_shape=(
            jax.ShapeDtypeStruct((members, slot_rows, LANES), jnp.float32),
            jax.ShapeDtypeStruct(rhs_local.shape[::-1], jnp.float32),
            jax.ShapeDtypeStruct((samples, couple_local.shape[1]), jnp.float32),
        ),
        in_specs=[HBM] * len(given),
        out_specs=(HBM, HBM, HBM),
        scratch_shapes=[
            *[like(array) for array in given[:3]],
            index_here,
            like(row_index),
            like(rhs_sep1),
            like(inv_sep1),
            update,
            wide,
            pltpu.VMEM((members, slot_rows, LANES), jnp.float32),
            pltpu.VMEM(rhs_local.shape[::-1], jnp.float32),
            pltpu.VMEM((samples, couple_local.shape[1]), jnp.float32),
            pltpu.SemaphoreType.DMA((10,)),
            pltpu.SemaphoreType.DMA((5,)),
        ],
        compiler_params=pltpu.CompilerParams(vmem_limit_bytes=63 * 2**20),
        name="local_forward",
    )(*given)
    inv_slots, root = pl.pallas_call(
        functools.partial(root_kernel, position),
        out_shape=(
            jax.ShapeDtypeStruct((members, inv_sep0.shape[0], LANES), jnp.float32),
            jax.ShapeDtypeStruct((members, depth, LANES), jnp.float32),
        ),
        in_specs=[VMEM, HBM, HBM, HBM],
        out_specs=(VMEM, VMEM),
        scratch_shapes=[
            index_here,
            like(row_index),
            like(rhs_sep0),
            like(inv_sep0),
            update,
            wide,
            pltpu.SemaphoreType.DMA((4,)),
        ],
        compiler_params=pltpu.CompilerParams(vmem_limit_bytes=24 * 2**20),
        name="local_root",
    )(lifted, row_index, rhs_sep0, inv_sep0)
    return slots, inv_slots, root, solved


def spread_rows(target, base, source):
    members, depth, _ = source.shape
    piles = lane_piles(LANES)
    step = LANES // depth
    for member in range(0, members, step):
        rows = source[member : member + step].reshape(LANES, LANES)
        for g in range(PILES):
            start = base + (g * members + member) * depth
            target[start : start + LANES, :] = jnp.where(piles == g, rows, 0.0)


def folded(wide):
    samples = LANES // PILES
    total_here = wide[:, :samples]
    for g in range(1, PILES):
        total_here = total_here + wide[:, g * samples : (g + 1) * samples]
    return total_here


def own_rows(table, start, rows):
    return folded(table[pl.ds(pl.multiple_of(start, rows), rows), :])


def gather_rows(target, source, index, first, last):
    @pl.loop(first, last)
    def _(step):
        base = pl.multiple_of(step * WIDE, WIDE)
        for k in range(WIDE):
            target[pl.ds(base + k, 1), :] = source[pl.ds(index[0, base + k], 1), :]


def backward_kernel(
    position, one, root, solved, inv, couple, index, x_local, own_one, own_root,
    one_here, root_here, solved_here, inv_here, couple_here, index_here, ancestor, above, sems,
):
    get_one, get_root, get_index, get_couple, get_solved, get_inv = fetch(
        [
            (one, one_here),
            (root, root_here),
            (index, index_here),
            (couple, couple_here),
            (solved, solved_here),
            (inv, inv_here),
        ],
        sems,
    )
    sep_rows = PILES * one.shape[0] * one.shape[1]
    rows_one = own_one.shape[0]
    rows_root = own_root.shape[0]
    get_one.wait()
    spread_rows(ancestor, 0, one_here)
    get_root.wait()
    spread_rows(ancestor, sep_rows, root_here)
    here = position()
    own_one[...] = own_rows(ancestor, here % (sep_rows // rows_one) * rows_one, rows_one)
    own_root[...] = own_rows(ancestor, sep_rows + here * rows_root, rows_root)
    get_index.wait()
    gather_rows(above, ancestor, index_here, 0, index.shape[1] // WIDE)
    get_couple.wait()
    get_solved.wait()
    held = halves(above[...])
    both = jnp.concatenate(held, axis=1)
    rows = couple_here.shape[0] // 4
    downs = []
    for k in range(4):
        high, low = halves(couple_here[k * rows : (k + 1) * rows, :])
        part = dot16(high, both)
        downs.append(folded(part[:, :LANES] + (part[:, LANES:] + dot16(low, held[0]))).T)
    rest = solved_here[...] - jnp.concatenate(downs, axis=1)
    get_inv.wait()
    x_local[...] = wide_product(rest, inv_here[...])


def backward(one, root, solved, inv_local, couple_local, row_index, rows_one, rows_root, position):
    samples = solved.shape[0]
    x_local, own_one, own_root = pl.pallas_call(
        functools.partial(backward_kernel, position),
        out_shape=(
            jax.ShapeDtypeStruct(solved.shape, jnp.float32),
            jax.ShapeDtypeStruct((rows_one, samples), jnp.float32),
            jax.ShapeDtypeStruct((rows_root, samples), jnp.float32),
        ),
        in_specs=[HBM] * 6,
        out_specs=(VMEM, VMEM, VMEM),
        scratch_shapes=[
            like(one),
            like(root),
            like(solved),
            like(inv_local),
            like(couple_local),
            pltpu.SMEM(row_index.shape, row_index.dtype),
            pltpu.VMEM((2 * PILES * one.shape[0] * one.shape[1], LANES), jnp.float32),
            pltpu.VMEM((couple_local.shape[1], LANES), jnp.float32),
            pltpu.SemaphoreType.DMA((6,)),
        ],
        compiler_params=pltpu.CompilerParams(vmem_limit_bytes=63 * 2**20),
        name="local_backward",
    )(one, root, solved, inv_local, couple_local, row_index)
    return x_local.T, own_one, own_root


def own_index():
    return own_position(EVERY)


def kernel_call(body, out_shapes, name, scratch=()):
    return pl.pallas_call(
        body,
        out_shape=tuple(jax.ShapeDtypeStruct(shape, jnp.float32) for shape in out_shapes),
        scratch_shapes=[pltpu.VMEM(shape, jnp.float32) for shape in scratch],
        compiler_params=pltpu.CompilerParams(vmem_limit_bytes=16 * 2**20),
        name=name,
    )


def summed(parts):
    terms = [parts[k] for k in range(parts.shape[0])]
    while len(terms) > 1:
        terms = [a + b for a, b in zip(terms[::2], terms[1::2], strict=True)]
    return terms[0]


def rows_of(piece):
    samples = LANES // PILES
    return jnp.concatenate([piece[:, g * samples : (g + 1) * samples] for g in range(PILES)], axis=0)


def piece_of(rows):
    depth = rows.shape[0] // PILES
    return jnp.concatenate([rows[g * depth : (g + 1) * depth] for g in range(PILES)], axis=1)


def inv_one_block(slots):
    piece = slots[:, slots.shape[1] - 8 :, :]
    return piece.reshape(piece.shape[0] * 8, LANES)


def inv_root_block(mixed):
    members = mixed.shape[0] // 8
    return jnp.concatenate([mixed[pl.ds(4 + i, members, stride=8), :] for i in range(4)], axis=0)


def twice(rows):
    blank = jnp.zeros_like(rows)
    return jnp.concatenate(
        [jnp.concatenate([rows, blank], axis=1), jnp.concatenate([blank, rows], axis=1)],
        axis=0,
    )


def solve_one_kernel(parts, slots, inv_slots, out, scratch):
    scratch[...] = tall_product(inv_one_block(slots), twice(rows_of(summed(parts))))
    members = scratch.shape[0] // 8
    out[...] = inv_slots[...]
    for i in range(4):
        pieces = [scratch[pl.ds(4 * h + i, members, stride=8), :] for h in range(2)]
        out[pl.ds(i, members, stride=8), :] = jnp.concatenate(pieces, axis=1)


def couple_up_kernel(parts, root, couple, out, solved):
    samples = LANES // PILES
    total_here = summed(parts)[: solved.shape[0]]
    solved[...] = total_here
    flipped = total_here.T
    order = [(g, h) for g in range(2) for h in range(2)]
    y = jnp.concatenate([flipped[(2 * h + g) * samples : (2 * h + g + 1) * samples] for g, h in order], axis=1)
    pile = couple.shape[1] // PILES
    members = LANES // root.shape[1]
    for first in range(0, pile, LANES):
        columns = [slice(g * pile + first, g * pile + first + LANES) for g in range(PILES)]
        lifted = wide_product(y, jnp.concatenate([couple[:, c] for c in columns], axis=1))
        lifted = jnp.concatenate([lifted[:, g * LANES : (g + 1) * LANES] for g in range(PILES)], axis=0).T
        some = slice(first // LANES * members, (first // LANES + 1) * members)
        out[some] = root[some] - lifted.reshape(members, *root.shape[1:])


def solve_root_kernel(parts, mixed, out):
    y = tall_product(inv_root_block(mixed), twice(rows_of(summed(parts))))
    rows = out.shape[0]
    out[...] = jnp.concatenate([y[:rows], y[rows:]], axis=1)


def lift_root_kernel(solved, mixed, out):
    half = LANES // 2
    samples = LANES // PILES
    flipped = solved[...].T
    y = jnp.concatenate([flipped[:half], flipped[half:]], axis=1)
    every = wide_product(y, inv_root_block(mixed))
    piece = piece_of((every[:samples, :half] + every[samples:, half:]).T)
    for member in range(out.shape[0]):
        out[member] = piece


def rest_one_kernel(root, solved, couple, out):
    samples = LANES // PILES
    rows, columns = couple.shape
    pile = columns // PILES
    stacked = jnp.concatenate([couple[:, g * pile : (g + 1) * pile] for g in range(PILES)], axis=0)
    every = wide_product(stacked, root[...].reshape(pile, LANES))
    down = every[:rows, :samples]
    for g in range(1, PILES):
        down = down + every[g * rows : (g + 1) * rows, g * samples : (g + 1) * samples]
    order = [(h, g) for h in range(2) for g in range(2)]
    out[...] = solved[...] - jnp.concatenate([down[8 * g + 4 * h : 8 * g + 4 * h + 4] for h, g in order], axis=1)


def lift_one_kernel(rest, slots, out, scratch):
    samples = LANES // PILES
    members = rest.shape[0] // 4
    for i in range(4):
        pieces = rest[pl.ds(i, members, stride=4), :]
        for h in range(2):
            scratch[pl.ds(4 * h + i, members, stride=8), :] = pieces[:, 2 * samples * h : 2 * samples * (h + 1)]
    every = wide_product(scratch[...].T, inv_one_block(slots))
    half = LANES // 2
    piece = piece_of((every[:samples, :half] + every[samples:, half:]).T)
    for member in range(out.shape[0]):
        out[member] = piece


def exchange(slots, axes):
    return lax.all_to_all(slots, axes, 0, 0)


def spread(value, axes):
    return exchange(jnp.broadcast_to(value[None], (lax.axis_size(axes),) + value.shape), axes)


def shards(
    rhs_local,
    inv_local,
    couple_local,
    row_index,
    rhs_sep1,
    inv_sep1,
    couple_sep1,
    rhs_sep0,
    inv_sep0,
):
    samples = rhs_local.shape[1]
    members = lax.axis_size(GROUP)
    rows_one, rows_root = rhs_sep1.shape[0], rhs_sep0.shape[0]
    piece = (inv_sep0.shape[1] // members // PILES, LANES)
    block_one = (members * rows_one * samples // LANES, LANES)
    block_root = (members * rows_root * samples // LANES, LANES)
    flat_one = (members * rows_one // 2, 2 * samples)

    slots, inv_slots, root, solved_local = forward(
        rhs_local, inv_local, couple_local, row_index, rhs_sep1, inv_sep1, rhs_sep0, inv_sep0, own_index
    )
    slots, inv_slots, root = lax.optimization_barrier((exchange(slots, GROUP), inv_slots, root))
    parts = spread(jnp.sum(slots[:, : piece[0]], axis=0), HALF)
    mixed = (members * inv_slots.shape[1], LANES)
    (parts,) = kernel_call(solve_one_kernel, [mixed], "solve_one", [flat_one])(parts, slots, inv_slots.reshape(mixed))
    parts = exchange(parts.reshape(members, -1, LANES), GROUP)
    mixed = parts.reshape(mixed)
    solved_shape = (block_one[0] // members, LANES)
    parts, solved_one = kernel_call(couple_up_kernel, [(members, *piece), solved_shape], "couple_up")(
        parts, root, couple_sep1
    )
    parts = spread(jnp.sum(exchange(parts, GROUP), axis=0), LINE)
    (parts,) = kernel_call(solve_root_kernel, [block_root], "solve_root")(parts, mixed)
    solved_root = jnp.sum(exchange(parts.reshape(members, -1, LANES), GROUP), axis=0)
    solved_root = spread(solved_root, GROUP).reshape(block_root)
    (parts,) = kernel_call(lift_root_kernel, [(lax.axis_size(LINE), *piece)], "lift_root")(solved_root, mixed)
    x_root = spread(jnp.sum(exchange(parts, LINE), axis=0), GROUP)
    (rest,) = kernel_call(rest_one_kernel, [solved_one.shape], "rest_one")(x_root, solved_one, couple_sep1)
    rest = spread(rest, GROUP).reshape(block_one)
    (parts,) = kernel_call(lift_one_kernel, [(lax.axis_size(HALF), *piece)], "lift_one", [flat_one])(rest, slots)
    x_one = spread(jnp.sum(exchange(parts, HALF), axis=0), GROUP)
    return backward(x_one, x_root, solved_local, inv_local, couple_local, row_index, rows_one, rows_root, own_index)


def solution(mesh):
    leaf, blk = mesh.devices.shape
    regrouped = Mesh(mesh.devices.reshape(2, leaf // 8, 2, 2, blk), EVERY)
    spec = P(EVERY, None)
    return jax.shard_map(shards, mesh=regrouped, in_specs=(spec,) * 9, out_specs=(spec,) * 3, check_vma=False)
```

```python
import functools

import jax
import jax.numpy as jnp
from jax import lax
from jax.experimental import pallas as pl
from jax.experimental.pallas import tpu as pltpu
from jax.sharding import Mesh
from jax.sharding import PartitionSpec as P

GROUP = ("near", "core", "blk")
HALF = ("pair",)
LINE = ("half", "pair")
EVERY = LINE + GROUP

VMEM = pl.BlockSpec(memory_space=pltpu.VMEM)
SMEM = pl.BlockSpec(memory_space=pltpu.SMEM)
HBM = pl.BlockSpec(memory_space=pltpu.HBM)
LANES = 128
UNROLL = 32
WIDE = 128


def halves(value):
    high = value.astype(jnp.bfloat16)
    return high, (value - high.astype(jnp.float32)).astype(jnp.bfloat16)


def dot16(left, right):
    return jnp.dot(left, right, preferred_element_type=jnp.float32)


def tall_product(left, right):
    n = right.shape[1]
    left_high, left_low = halves(left)
    right_high, right_low = halves(right)
    both = dot16(left_high, jnp.concatenate([right_high, right_low], axis=1))
    return both[:, :n] + (both[:, n:] + dot16(left_low, right_high))


def wide_product(left, right):
    m = left.shape[0]
    left_high, left_low = halves(left)
    right_high, right_low = halves(right)
    both = dot16(jnp.concatenate([left_high, left_low], axis=0), right_high)
    return both[:m] + (both[m:] + dot16(left_high, right_low))


PILES = 4


def lane_piles(rows):
    return lax.broadcasted_iota(jnp.int32, (rows, LANES), 1) // (LANES // PILES)


def deal(stacks, width):
    granule = lax.broadcasted_iota(jnp.int32, stacks[0].shape, 1) // width
    turned = [stack if k == 0 else pltpu.roll(stack, width * k, 1) for k, stack in enumerate(stacks)]
    count = LANES // width
    for first in range(count):
        row = jnp.zeros_like(stacks[0])
        for k, stack in enumerate(turned):
            row = jnp.where(granule == (first + k) % count, stack, row)
        yield row if first == 0 else pltpu.roll(row, LANES - width * first, 1)


def fetch(pairs, sems):
    copies = [pltpu.make_async_copy(source, target, sems.at[k]) for k, (source, target) in enumerate(pairs)]
    for copy in copies:
        copy.start()
    return copies


def own_position(axes):
    position = lax.axis_index(axes[0])
    for axis in axes[1:]:
        position = position * lax.axis_size(axis) + lax.axis_index(axis)
    return position


def forward_kernel(
    position, rhs, inv, couple, index, rhs_one, inv_one, slots, solved, lifted_out,
    rhs_here, inv_here, couple_here, index_here, index_wide, rhs_one_here, inv_one_here, update, lifted,
    slots_here, solved_here, lifted_here, sems, out_sems,
):
    quarter = couple.shape[1] // 4
    quarters = [slice(k * quarter, (k + 1) * quarter) for k in range(4)]
    copies = fetch(
        [
            (index, index_here),
            (index, index_wide),
            (inv_one, inv_one_here),
            (rhs, rhs_here),
            (inv, inv_here),
            *[(couple.at[:, columns], couple_here.at[:, columns]) for columns in quarters],
            (rhs_one, rhs_one_here),
        ],
        sems,
    )
    get_index, get_index_wide, get_inv_one, get_rhs, get_inv, *get_couple, get_rhs_one = copies
    samples = rhs.shape[0]
    rows_one = rhs_one.shape[0]
    sep_rows = inv_one.shape[1]
    pile = sep_rows // PILES
    depth = slots.shape[1] - rows_one // 2
    clear(update, 0, sep_rows)

    get_index.wait()
    get_index_wide.wait()
    low = jnp.sum((index_wide[...] < sep_rows).astype(jnp.int32))
    get_inv_one.wait()
    for first in range(0, pile, LANES):
        columns = [slice(g * pile + first, g * pile + first + LANES) for g in range(PILES)]
        stacks = [inv_one_here[r : r + rows_one // 2, c] for r in (0, rows_one // 2) for c in columns]
        for k, row in enumerate(deal(stacks, depth)):
            slots_here[first // depth + k, depth:, :] = row
    puts = fetch([(slots_here.at[:, depth:, :], slots.at[:, depth:, :])], out_sems.at[:1])

    get_rhs.wait()
    get_inv.wait()
    y = tall_product(inv_here[...], rhs_here[...].T).T
    solved_here[...] = y
    puts += fetch([(solved_here, solved)], out_sems.at[1:2])
    y = -y
    for copy, columns in zip(get_couple, quarters, strict=True):
        copy.wait()
        part = wide_product(y, couple_here[:, columns])
        lifted_here[:, columns] = part
        lifted[columns, :] = jnp.concatenate([part] * PILES, axis=0).T

    puts += fetch([(lifted_here, lifted_out)], out_sems.at[2:3])

    scatter_rows(update, lifted, index_here, 0, (low + UNROLL - 1) // UNROLL)

    get_rhs_one.wait()
    own_one = pl.ds(pl.multiple_of(position() % (sep_rows // rows_one) * rows_one, rows_one), rows_one)
    update[own_one, :] = update[own_one, :] + jnp.concatenate([rhs_one_here[...]] * PILES, axis=1)
    members = slots.shape[0]
    for k in range(2):
        some = slice(k * members // 2, (k + 1) * members // 2)
        for member in range(some.start, some.stop):
            slots_here[member, :depth, :] = merged(update, 0, member, depth, pile)
        puts += fetch([(slots_here.at[some, :depth, :], slots.at[some, :depth, :])], out_sems.at[3 + k : 4 + k])
    for put in puts:
        put.wait()


def clear(target, start, rows):
    @pl.loop(0, rows // 512)
    def _(step):
        target[pl.ds(pl.multiple_of(start + step * 512, 512), 512), :] = jnp.zeros((512, LANES), jnp.float32)


def scatter_rows(target, source, index, first, last):
    @pl.loop(first, last)
    def _(step):
        base = pl.multiple_of(step * UNROLL, UNROLL)
        for k in range(UNROLL):
            target[pl.ds(index[0, base + k], 1), :] = source[pl.ds(base + k, 1), :]


def merged(update, base, member, depth, pile):
    starts = [base + g * pile + member * depth for g in range(PILES)]
    piles = lane_piles(depth)
    piece = update[starts[0] : starts[0] + depth, :]
    for g in range(1, PILES):
        piece = jnp.where(piles == g, update[starts[g] : starts[g] + depth, :], piece)
    return piece


def root_kernel(
    position, lifted_wide, index, rhs_root, inv_root, inv_slots, root,
    index_here, index_wide, rhs_root_here, inv_root_here, update, lifted, sems,
):
    copies = fetch(
        [(index, index_here), (index, index_wide), (rhs_root, rhs_root_here), (inv_root, inv_root_here)], sems
    )
    rows_root = rhs_root.shape[0]
    sep_rows = inv_root.shape[1]
    pile = sep_rows // PILES
    depth = root.shape[1]
    clear(update, sep_rows, sep_rows)
    lifted[...] = jnp.concatenate([lifted_wide[...]] * PILES, axis=0).T
    for copy in copies:
        copy.wait()
    low = jnp.sum((index_wide[...] < sep_rows).astype(jnp.int32))
    scatter_rows(update, lifted, index_here, low // UNROLL, index.shape[1] // UNROLL)
    own_root = pl.ds(pl.multiple_of(sep_rows + position() * rows_root, rows_root), rows_root)
    update[own_root, :] = update[own_root, :] + jnp.concatenate([rhs_root_here[...]] * PILES, axis=1)
    for member in range(root.shape[0]):
        root[member] = merged(update, sep_rows, member, depth, pile)
    for first in range(0, pile, LANES):
        columns = [slice(g * pile + first, g * pile + first + LANES) for g in range(PILES)]
        stacks = [inv_root_here[r : r + rows_root // 2, c] for r in (0, rows_root // 2) for c in columns]
        for k, row in enumerate(deal(stacks, depth)):
            inv_slots[first // depth + k, rows_root // 2 :, :] = row


def like(array):
    return pltpu.VMEM(array.shape, array.dtype)


def forward(rhs_local, inv_local, couple_local, row_index, rhs_sep1, inv_sep1, rhs_sep0, inv_sep0, position):
    samples = rhs_local.shape[1]
    members = lax.axis_size(GROUP)
    depth = inv_sep1.shape[1] // members // PILES
    slot_rows = depth + inv_sep1.shape[0] // 2
    given = (rhs_local.T, inv_local, couple_local, row_index, rhs_sep1, inv_sep1)
    wide = pltpu.VMEM((couple_local.shape[1], LANES), jnp.float32)
    update = pltpu.VMEM((2 * inv_sep1.shape[1], LANES), jnp.float32)
    index_here = pltpu.SMEM(row_index.shape, row_index.dtype)
    slots, solved, lifted = pl.pallas_call(
        functools.partial(forward_kernel, position),
        out_shape=(
            jax.ShapeDtypeStruct((members, slot_rows, LANES), jnp.float32),
            jax.ShapeDtypeStruct(rhs_local.shape[::-1], jnp.float32),
            jax.ShapeDtypeStruct((samples, couple_local.shape[1]), jnp.float32),
        ),
        in_specs=[HBM] * len(given),
        out_specs=(HBM, HBM, HBM),
        scratch_shapes=[
            *[like(array) for array in given[:3]],
            index_here,
            like(row_index),
            like(rhs_sep1),
            like(inv_sep1),
            update,
            wide,
            pltpu.VMEM((members, slot_rows, LANES), jnp.float32),
            pltpu.VMEM(rhs_local.shape[::-1], jnp.float32),
            pltpu.VMEM((samples, couple_local.shape[1]), jnp.float32),
            pltpu.SemaphoreType.DMA((10,)),
            pltpu.SemaphoreType.DMA((5,)),
        ],
        compiler_params=pltpu.CompilerParams(vmem_limit_bytes=63 * 2**20),
        name="local_forward",
    )(*given)
    inv_slots, root = pl.pallas_call(
        functools.partial(root_kernel, position),
        out_shape=(
            jax.ShapeDtypeStruct((members, inv_sep0.shape[0], LANES), jnp.float32),
            jax.ShapeDtypeStruct((members, depth, LANES), jnp.float32),
        ),
        in_specs=[VMEM, HBM, HBM, HBM],
        out_specs=(VMEM, VMEM),
        scratch_shapes=[
            index_here,
            like(row_index),
            like(rhs_sep0),
            like(inv_sep0),
            update,
            wide,
            pltpu.SemaphoreType.DMA((4,)),
        ],
        compiler_params=pltpu.CompilerParams(vmem_limit_bytes=24 * 2**20),
        name="local_root",
    )(lifted, row_index, rhs_sep0, inv_sep0)
    return slots, inv_slots, root, solved


def spread_rows(target, base, source):
    members, depth, _ = source.shape
    piles = lane_piles(LANES)
    step = LANES // depth
    for member in range(0, members, step):
        rows = source[member : member + step].reshape(LANES, LANES)
        for g in range(PILES):
            start = base + (g * members + member) * depth
            target[start : start + LANES, :] = jnp.where(piles == g, rows, 0.0)


def folded(wide):
    samples = LANES // PILES
    total_here = wide[:, :samples]
    for g in range(1, PILES):
        total_here = total_here + wide[:, g * samples : (g + 1) * samples]
    return total_here


def own_rows(table, start, rows):
    return folded(table[pl.ds(pl.multiple_of(start, rows), rows), :])


def gather_rows(target, source, index, first, last):
    @pl.loop(first, last)
    def _(step):
        base = pl.multiple_of(step * WIDE, WIDE)
        for k in range(WIDE):
            target[pl.ds(base + k, 1), :] = source[pl.ds(index[0, base + k], 1), :]


def backward_kernel(
    position, one, root, solved, inv, couple, index, x_local, own_one, own_root,
    one_here, root_here, solved_here, inv_here, couple_here, index_here, ancestor, above, sems,
):
    get_one, get_root, get_index, get_couple, get_solved, get_inv = fetch(
        [
            (one, one_here),
            (root, root_here),
            (index, index_here),
            (couple, couple_here),
            (solved, solved_here),
            (inv, inv_here),
        ],
        sems,
    )
    sep_rows = PILES * one.shape[0] * one.shape[1]
    rows_one = own_one.shape[0]
    rows_root = own_root.shape[0]
    get_one.wait()
    spread_rows(ancestor, 0, one_here)
    get_root.wait()
    spread_rows(ancestor, sep_rows, root_here)
    get_index.wait()
    gather_rows(above, ancestor, index_here, 0, index.shape[1] // WIDE)
    get_couple.wait()
    get_solved.wait()
    here = position()
    own_one[...] = own_rows(ancestor, here % (sep_rows // rows_one) * rows_one, rows_one)
    own_root[...] = own_rows(ancestor, sep_rows + here * rows_root, rows_root)
    held = halves(above[...])
    both = jnp.concatenate(held, axis=1)
    rows = couple_here.shape[0] // 4
    downs = []
    for k in range(4):
        high, low = halves(couple_here[k * rows : (k + 1) * rows, :])
        part = dot16(high, both)
        downs.append(folded(part[:, :LANES] + (part[:, LANES:] + dot16(low, held[0]))).T)
    rest = solved_here[...] - jnp.concatenate(downs, axis=1)
    get_inv.wait()
    x_local[...] = wide_product(rest, inv_here[...])


def backward(one, root, solved, inv_local, couple_local, row_index, rows_one, rows_root, position):
    samples = solved.shape[0]
    x_local, own_one, own_root = pl.pallas_call(
        functools.partial(backward_kernel, position),
        out_shape=(
            jax.ShapeDtypeStruct(solved.shape, jnp.float32),
            jax.ShapeDtypeStruct((rows_one, samples), jnp.float32),
            jax.ShapeDtypeStruct((rows_root, samples), jnp.float32),
        ),
        in_specs=[HBM] * 6,
        out_specs=(VMEM, VMEM, VMEM),
        scratch_shapes=[
            like(one),
            like(root),
            like(solved),
            like(inv_local),
            like(couple_local),
            pltpu.SMEM(row_index.shape, row_index.dtype),
            pltpu.VMEM((2 * PILES * one.shape[0] * one.shape[1], LANES), jnp.float32),
            pltpu.VMEM((couple_local.shape[1], LANES), jnp.float32),
            pltpu.SemaphoreType.DMA((6,)),
        ],
        compiler_params=pltpu.CompilerParams(vmem_limit_bytes=63 * 2**20),
        name="local_backward",
    )(one, root, solved, inv_local, couple_local, row_index)
    return x_local.T, own_one, own_root


def own_index():
    return own_position(EVERY)


def kernel_call(body, out_shapes, name, scratch=()):
    return pl.pallas_call(
        body,
        out_shape=tuple(jax.ShapeDtypeStruct(shape, jnp.float32) for shape in out_shapes),
        scratch_shapes=[pltpu.VMEM(shape, jnp.float32) for shape in scratch],
        compiler_params=pltpu.CompilerParams(vmem_limit_bytes=16 * 2**20),
        name=name,
    )


def summed(parts):
    terms = [parts[k] for k in range(parts.shape[0])]
    while len(terms) > 1:
        terms = [a + b for a, b in zip(terms[::2], terms[1::2], strict=True)]
    return terms[0]


def rows_of(piece):
    samples = LANES // PILES
    return jnp.concatenate([piece[:, g * samples : (g + 1) * samples] for g in range(PILES)], axis=0)


def piece_of(rows):
    depth = rows.shape[0] // PILES
    return jnp.concatenate([rows[g * depth : (g + 1) * depth] for g in range(PILES)], axis=1)


def inv_one_block(slots):
    piece = slots[:, slots.shape[1] - 8 :, :]
    return piece.reshape(piece.shape[0] * 8, LANES)


def inv_root_block(mixed):
    members = mixed.shape[0] // 8
    return jnp.concatenate([mixed[pl.ds(4 + i, members, stride=8), :] for i in range(4)], axis=0)


def twice(rows):
    blank = jnp.zeros_like(rows)
    return jnp.concatenate(
        [jnp.concatenate([rows, blank], axis=1), jnp.concatenate([blank, rows], axis=1)],
        axis=0,
    )


def solve_one_kernel(parts, slots, inv_slots, out, scratch):
    scratch[...] = tall_product(inv_one_block(slots), twice(rows_of(summed(parts))))
    members = scratch.shape[0] // 8
    out[...] = inv_slots[...]
    for i in range(4):
        pieces = [scratch[pl.ds(4 * h + i, members, stride=8), :] for h in range(2)]
        out[pl.ds(i, members, stride=8), :] = jnp.concatenate(pieces, axis=1)


def couple_up_kernel(parts, root, couple, out, solved):
    samples = LANES // PILES
    total_here = summed(parts)[: solved.shape[0]]
    solved[...] = total_here
    flipped = total_here.T
    order = [(g, h) for g in range(2) for h in range(2)]
    y = jnp.concatenate([flipped[(2 * h + g) * samples : (2 * h + g + 1) * samples] for g, h in order], axis=1)
    pile = couple.shape[1] // PILES
    members = LANES // root.shape[1]
    for first in range(0, pile, LANES):
        columns = [slice(g * pile + first, g * pile + first + LANES) for g in range(PILES)]
        lifted = wide_product(y, jnp.concatenate([couple[:, c] for c in columns], axis=1))
        lifted = jnp.concatenate([lifted[:, g * LANES : (g + 1) * LANES] for g in range(PILES)], axis=0).T
        some = slice(first // LANES * members, (first // LANES + 1) * members)
        out[some] = root[some] - lifted.reshape(members, *root.shape[1:])


def solve_root_kernel(parts, mixed, out):
    y = tall_product(inv_root_block(mixed), twice(rows_of(summed(parts))))
    rows = out.shape[0]
    out[...] = jnp.concatenate([y[:rows], y[rows:]], axis=1)


def lift_root_kernel(solved, mixed, out):
    half = LANES // 2
    samples = LANES // PILES
    flipped = solved[...].T
    y = jnp.concatenate([flipped[:half], flipped[half:]], axis=1)
    every = wide_product(y, inv_root_block(mixed))
    piece = piece_of((every[:samples, :half] + every[samples:, half:]).T)
    for member in range(out.shape[0]):
        out[member] = piece


def rest_one_kernel(root, solved, couple, out):
    samples = LANES // PILES
    rows, columns = couple.shape
    pile = columns // PILES
    stacked = jnp.concatenate([couple[:, g * pile : (g + 1) * pile] for g in range(PILES)], axis=0)
    every = wide_product(stacked, root[...].reshape(pile, LANES))
    down = every[:rows, :samples]
    for g in range(1, PILES):
        down = down + every[g * rows : (g + 1) * rows, g * samples : (g + 1) * samples]
    order = [(h, g) for h in range(2) for g in range(2)]
    out[...] = solved[...] - jnp.concatenate([down[8 * g + 4 * h : 8 * g + 4 * h + 4] for h, g in order], axis=1)


def lift_one_kernel(rest, slots, out, scratch):
    samples = LANES // PILES
    members = rest.shape[0] // 4
    for i in range(4):
        pieces = rest[pl.ds(i, members, stride=4), :]
        for h in range(2):
            scratch[pl.ds(4 * h + i, members, stride=8), :] = pieces[:, 2 * samples * h : 2 * samples * (h + 1)]
    every = wide_product(scratch[...].T, inv_one_block(slots))
    half = LANES // 2
    piece = piece_of((every[:samples, :half] + every[samples:, half:]).T)
    for member in range(out.shape[0]):
        out[member] = piece


def exchange(slots, axes):
    return lax.all_to_all(slots, axes, 0, 0)


def spread(value, axes):
    return exchange(jnp.broadcast_to(value[None], (lax.axis_size(axes),) + value.shape), axes)


def shards(
    rhs_local,
    inv_local,
    couple_local,
    row_index,
    rhs_sep1,
    inv_sep1,
    couple_sep1,
    rhs_sep0,
    inv_sep0,
):
    samples = rhs_local.shape[1]
    members = lax.axis_size(GROUP)
    rows_one, rows_root = rhs_sep1.shape[0], rhs_sep0.shape[0]
    piece = (inv_sep0.shape[1] // members // PILES, LANES)
    block_one = (members * rows_one * samples // LANES, LANES)
    block_root = (members * rows_root * samples // LANES, LANES)
    flat_one = (members * rows_one // 2, 2 * samples)

    slots, inv_slots, root, solved_local = forward(
        rhs_local, inv_local, couple_local, row_index, rhs_sep1, inv_sep1, rhs_sep0, inv_sep0, own_index
    )
    slots, inv_slots, root = lax.optimization_barrier((exchange(slots, GROUP), inv_slots, root))
    parts = spread(jnp.sum(slots[:, : piece[0]], axis=0), HALF)
    mixed = (members * inv_slots.shape[1], LANES)
    (parts,) = kernel_call(solve_one_kernel, [mixed], "solve_one", [flat_one])(parts, slots, inv_slots.reshape(mixed))
    parts = exchange(parts.reshape(members, -1, LANES), GROUP)
    mixed = parts.reshape(mixed)
    solved_shape = (block_one[0] // members, LANES)
    parts, solved_one = kernel_call(couple_up_kernel, [(members, *piece), solved_shape], "couple_up")(
        parts, root, couple_sep1
    )
    parts = spread(jnp.sum(exchange(parts, GROUP), axis=0), LINE)
    (parts,) = kernel_call(solve_root_kernel, [block_root], "solve_root")(parts, mixed)
    solved_root = jnp.sum(exchange(parts.reshape(members, -1, LANES), GROUP), axis=0)
    solved_root = spread(solved_root, GROUP).reshape(block_root)
    (parts,) = kernel_call(lift_root_kernel, [(lax.axis_size(LINE), *piece)], "lift_root")(solved_root, mixed)
    x_root = spread(jnp.sum(exchange(parts, LINE), axis=0), GROUP)
    (rest,) = kernel_call(rest_one_kernel, [solved_one.shape], "rest_one")(x_root, solved_one, couple_sep1)
    rest = spread(rest, GROUP).reshape(block_one)
    (parts,) = kernel_call(lift_one_kernel, [(lax.axis_size(HALF), *piece)], "lift_one", [flat_one])(rest, slots)
    x_one = spread(jnp.sum(exchange(parts, HALF), axis=0), GROUP)
    return backward(x_one, x_root, solved_local, inv_local, couple_local, row_index, rows_one, rows_root, own_index)


def solution(mesh):
    leaf, blk = mesh.devices.shape
    regrouped = Mesh(mesh.devices.reshape(2, leaf // 8, 2, 2, blk), EVERY)
    spec = P(EVERY, None)
    return jax.shard_map(shards, mesh=regrouped, in_specs=(spec,) * 9, out_specs=(spec,) * 3, check_vma=False)
```
